32 devices in a mesh: dp: 8 (over z, y), seq: 4 (over x, core).
Axes of the slice: x: 2, y: 2, z: 4, core: 2. Of those that a mesh axis runs over, the one named last changes fastest.
Arguments:
- bases: int32 [8, 6144], P('dp', 'seq'), may hold values from 0 to 3
- embed_weight: bfloat16 [15, 4, 768], P(None, None, 'dp'), may hold values from -1.5 to 1.5
- embed_bias: bfloat16 [768], P('dp'), may hold values from -3 to 3
- norm_gain: bfloat16 [768], P('dp'), may hold values from 0.5 to 1.5
- proj_weight: bfloat16 [768, 896], P('dp'), may hold values from -0.21875 to 0.21875
- proj_bias: bfloat16 [896], P('dp'), may hold values from -3 to 3
- cotangent: bfloat16 [8, 3072, 896], P('dp', 'seq'), may hold values from -6 to 6
Outputs:
- pooled: bfloat16 [8, 3072, 896], P('dp', 'seq')
- grad_embed_weight: float32 [15, 4, 768], P(None, None, 'dp')
- grad_embed_bias: float32 [768], P('dp')
- grad_norm_gain: float32 [768], P('dp')
- grad_proj_weight: float32 [768, 896], P('dp')
- grad_proj_bias: float32 [896], P('dp')
The draws below stay inside these ranges and needn't reach their ends.
All inputs are finite; a program needn't handle non-finite values.
Results may differ from the reference program's by a relative error of at most 0.0065.
Values may be sent and summed in bfloat16 or wider, within the bound.
A program may use at most 64 MiB of HBM per device.

```python
import jax
import jax.numpy as jnp
from jax import lax

D0 = 768
D1 = 896
KW = 15
SEQ = 6144
BATCH = 8


def plant(result, own_key, smallest, largest):
    dims = result.shape
    place = [jax.random.randint(jax.random.fold_in(own_key, axis), (), 0, dims[axis]) for axis in range(len(dims))]
    result = result.at[tuple(place)].set(smallest)
    longest = dims.index(max(dims))
    place[longest] = (place[longest] + 1) % dims[longest]
    return result.at[tuple(place)].set(largest)


def raised(result, key, source, target, shards_of, factor):
    def block_of(position):
        return (jnp.arange(result.shape[position]) // (result.shape[position] // shards_of)).reshape((-1,) + (1,) * (result.ndim - 1 - position))

    one_side = jax.random.permutation(key, shards_of)[block_of(target)]
    second = (block_of(target) + shards_of // 2) % shards_of
    return jnp.where((block_of(source) == one_side) | (block_of(source) == second), factor * result, result)


def levels(own_key, shape, split, least, high):
    level, own = 1.0, jax.random.fold_in(own_key, 6)
    for axis_at, blocks in split:
        draws = jnp.exp(jax.random.uniform(jax.random.fold_in(own, axis_at), (blocks,), jnp.float32, least / len(split), high / len(split)))
        level = level * jnp.repeat(draws, shape[axis_at] // blocks).reshape([-1 if axis == axis_at else 1 for axis in range(len(shape))])
    return level


def scatter_about(stream_key, dims, spread, reach, pieces=(), kind=jnp.bfloat16):
    drawn = jax.random.normal(stream_key, dims, jnp.float32) * spread
    if len(pieces) > 0:
        drawn = levels(stream_key, dims, pieces, -0.22, 0.18) * drawn
    return jnp.clip(drawn, min=-reach, max=reach).astype(kind)


def heavy_noise(rng, shape, spread, most, cuts, heavy, held_as=jnp.bfloat16):
    drawn = spread * jax.random.normal(rng, shape, jnp.float32)
    if cuts:
        drawn = drawn * levels(rng, shape, cuts, -0.22, 0.18)
    return jnp.clip(raised(drawn, jax.random.fold_in(rng, 3), *heavy), -most, most).astype(held_as)


def setup_inputs(seed: int = 0) -> dict:
    arg_keys = jax.random.split(jax.random.key(seed), 8)
    return {
        "bases": plant(jax.random.randint(arg_keys[0], (BATCH, SEQ), 0, 4), jax.random.fold_in(arg_keys[0], 1), 0, 3).astype(jnp.int32),
        "embed_weight": scatter_about(arg_keys[1], (KW, 4, D0), KW ** -0.5, 1.5, ((2, 8),)),
        "embed_bias": scatter_about(arg_keys[2], (D0,), 0.5, 3.0, ((0, 8),)),
        "norm_gain": jnp.clip(1.0 + 0.1 * jax.random.normal(arg_keys[3], (D0,), jnp.float32), 0.5, 1.5).astype(jnp.bfloat16),
        "proj_weight": scatter_about(arg_keys[4], (D0, D1), D0 ** -0.5, 0.21875, ((0, 8),)),
        "proj_bias": scatter_about(arg_keys[5], (D1,), 0.5, 3.0, ((0, 8),)),
        "cotangent": heavy_noise(arg_keys[6], (BATCH, SEQ // 2, D1), 1.0, 6.0, ((0, 8), (1, 4)), (0, 2, 8, 2.0)),
    }


def sample_pass(codes, cotan, embed_weight, embed_bias, norm_gain, proj_weight, proj_bias, scale_factor):
    kernel_width = embed_weight.shape[0]
    row_count = cotan.shape[0] * 2
    letters = jnp.arange(1, 5, dtype=jnp.int32)
    features = jnp.concatenate([(codes[k:k + row_count, None] == letters).astype(jnp.bfloat16) for k in range(kernel_width)], axis=1)
    flat_weight = embed_weight.reshape(kernel_width * 4, -1)
    embedded = (jnp.dot(features, flat_weight, preferred_element_type=jnp.float32) + embed_bias.astype(jnp.float32)).astype(jnp.bfloat16)
    values = embedded.astype(jnp.float32)
    inverse = lax.rsqrt(lax.optimization_barrier(jnp.mean(values * values, axis=1, keepdims=True)) + 1e-06)
    scaled = values * inverse
    normed = scaled * norm_gain.astype(jnp.float32)
    activated = jax.nn.gelu(normed, approximate=True).astype(jnp.bfloat16)
    mixed = jnp.dot(activated, proj_weight, preferred_element_type=jnp.float32) + proj_bias.astype(jnp.float32)
    pooled = lax.optimization_barrier(jnp.mean(mixed.reshape(row_count // 2, 2, -1), axis=1)).astype(jnp.bfloat16)
    grad_mixed = (jnp.repeat(cotan.astype(jnp.float32), 2, axis=0) * scale_factor).astype(jnp.bfloat16)
    grad_proj_weight = lax.dot_general(activated, grad_mixed, (((0,), (0,)), ((), ())), preferred_element_type=jnp.float32)
    grad_proj_bias = lax.optimization_barrier(jnp.sum(grad_mixed.astype(jnp.float32), axis=0))
    grad_activated = lax.dot_general(grad_mixed, proj_weight, (((1,), (1,)), ((), ())), preferred_element_type=jnp.float32)
    _, pullback = jax.vjp(lambda v: jax.nn.gelu(v, approximate=True), normed)
    grad_normed = pullback(grad_activated)[0]
    grad_norm_gain = lax.optimization_barrier(jnp.sum(grad_normed * scaled, axis=0))
    weighted = grad_normed * norm_gain.astype(jnp.float32)
    grad_embedded = (inverse * (weighted - scaled * lax.optimization_barrier(jnp.mean(weighted * scaled, axis=1, keepdims=True)))).astype(jnp.bfloat16)
    grad_embed_weight = lax.dot_general(features, grad_embedded, (((0,), (0,)), ((), ())), preferred_element_type=jnp.float32).reshape(kernel_width, 4, -1)
    grad_embed_bias = lax.optimization_barrier(jnp.sum(grad_embedded.astype(jnp.float32), axis=0))
    return (pooled, (grad_embed_weight, grad_embed_bias, grad_norm_gain, grad_proj_weight, grad_proj_bias))

def reference(bases, embed_weight, embed_bias, norm_gain, proj_weight, proj_bias, cotangent):
    half_width = KW // 2
    codes = jnp.pad(bases + 1, ((0, 0), (half_width, half_width))).astype(jnp.int32)
    scale_factor = 0.5 / (BATCH * SEQ)
    initial = (jnp.zeros((KW, 4, D0), jnp.float32), jnp.zeros((D0,), jnp.float32), jnp.zeros((D0,), jnp.float32), jnp.zeros((D0, D1), jnp.float32), jnp.zeros((D1,), jnp.float32))

    def step(carry, inputs):
        pooled, grads = sample_pass(inputs[0], inputs[1], embed_weight, embed_bias, norm_gain, proj_weight, proj_bias, scale_factor)
        return (tuple((c + g for c, g in zip(carry, grads))), pooled)
    totals, pooled = lax.scan(step, initial, (codes, cotangent))
    return (pooled, totals[0], totals[1], totals[2], totals[3], totals[4])
```

```python
import functools

import jax
import jax.numpy as jnp
from jax import lax
from jax.experimental import pallas as pl
from jax.experimental.pallas import tpu as pltpu
from jax.sharding import PartitionSpec as P

F32, BF16 = jnp.float32, jnp.bfloat16
CUBIC = 0.044715
ROOT = 0.7978845608028654
NT = (((1,), (1,)), ((), ()))
TN = (((0,), (0,)), ((), ()))


def dot(a, b, dims):
    return lax.dot_general(a, b, dims, preferred_element_type=F32)


def build_features(codes_ref, halo_ref, stack_ref, feat_ref, kernel_width):
    half = codes_ref.shape[1]
    ext = jnp.concatenate([halo_ref[0], codes_ref[...], halo_ref[1]], axis=1)
    total = half + 256
    for parity in range(2):
        for k in range(kernel_width):
            source = parity + k - kernel_width // 2
            row, shift = source % 2, (source - source % 2) // 2
            moved = ext if shift == 0 else pltpu.roll(ext, (-shift) % total, 1)
            stack_ref[parity, k : k + 1, :] = moved[row : row + 1, 128 : 128 + half]
        stack_ref[parity, kernel_width : kernel_width + 1, :] = jnp.ones((1, half), jnp.int32)
        stack = stack_ref[parity]
        for c in range(4):
            feat_ref[parity, 16 * c : 16 * c + 16, :] = (
                jnp.where(stack == c + 1, 1.0, 0.0).astype(BF16)
            )


def pick_row(lane, packed):
    lanes = lax.broadcasted_iota(jnp.int32, (16, 128), 1)
    onehot = jnp.where(lanes == lane, 1.0, 0.0).astype(BF16)
    return dot(onehot, packed, NT)[0:1]


def forward_chunk(start, size, feat_ref, weight, gain, scaled_ref, slope_ref, inv_ref, pact_ref):
    total = None
    for parity in range(2):
        features = feat_ref[parity, :, pl.ds(start, size)]
        emb = dot(features, weight, (((0,), (1,)), ((), ())))
        emb = emb.astype(BF16).astype(F32)
        inverse = lax.rsqrt(jnp.mean(emb * emb, axis=1, keepdims=True) + 1e-6)
        scaled = emb * inverse
        x = scaled * gain
        sq = x * x
        t = jnp.tanh(x * (ROOT + (ROOT * CUBIC) * sq))
        half_x = 0.5 * x
        act = half_x + half_x * t
        half_t = 0.5 + 0.5 * t
        slope = half_t + half_x * (1.0 - t * t) * (ROOT + (3.0 * ROOT * CUBIC) * sq)
        scaled_ref[parity, pl.ds(start, size), :] = scaled
        slope_ref[parity, pl.ds(start, size), :] = slope
        inv_ref[parity, pl.ds(start, size), :] = jnp.broadcast_to(inverse, (size, 128))
        total = act if total is None else total + act
    pact_ref[pl.ds(start, size), :] = total.astype(BF16)


def backward_chunk(start, size, cot_ref, w, gain, scaled_ref, slope_ref, inv_ref, ge_ref, gain_acc):
    ga = dot(cot_ref[pl.ds(start, size), :], w, NT)
    width = ga.shape[1]
    for parity in range(2):
        scaled = scaled_ref[parity, pl.ds(start, size), :]
        inverse = inv_ref[parity, pl.ds(start, size), 0:1]
        u = ga * slope_ref[parity, pl.ds(start, size), :]
        q = u * scaled
        gain_acc[...] += jnp.sum(q.reshape(size // 8, 8, width), axis=0)
        mean = jnp.sum(q * gain, axis=1, keepdims=True) * (1.0 / width)
        ge = inverse * (u * gain - scaled * mean)
        ge_ref[parity, pl.ds(start, size), :] = ge.astype(BF16)


def small_grads(feat_ref, ge_ref, cot_ref, gain_acc, put):
    g = dot(feat_ref[0], ge_ref[0], (((1,), (0,)), ((), ())))
    g = g + dot(feat_ref[1], ge_ref[1], (((1,), (0,)), ((), ())))
    width = g.shape[1]
    gain_row = jnp.sum(gain_acc[...], axis=0, keepdims=True)
    rows = lax.broadcasted_iota(jnp.int32, (64, width), 0)
    low = jnp.where(rows == 0, gain_row, 0.0)
    channels = jnp.concatenate([g, low], axis=0).T
    ones = jnp.ones((16, cot_ref.shape[0]), BF16)
    pb = 2.0 * dot(ones, cot_ref[...], (((1,), (0,)), ((), ())))[0:1]
    rows = lax.broadcasted_iota(jnp.int32, (128, pb.shape[1]), 0)
    biases = jnp.where(rows == 65, pb, 0.0).T
    return channels, biases


def local_kernel(dp, kernel_width, codes_ref, halo_ref, packed_ref, w_ref, cot_ref,
                 pooled_ref, gw_ref, small_ref,
                 stack, feat, scaled, slope, inv, pact, ge, gain_acc):
    half = codes_ref.shape[1]
    d0, d1 = w_ref.shape
    part0, part1 = d0 // dp, d1 // dp
    build_features(codes_ref, halo_ref, stack, feat, kernel_width)
    channels = jnp.concatenate([packed_ref[d, :part0, :] for d in range(dp)], axis=0)
    weight = channels[:, :64]
    gain = pick_row(64, channels)
    bias = pick_row(65, jnp.concatenate([packed_ref[d] for d in range(dp)], axis=0))
    gain_acc[...] = jnp.zeros_like(gain_acc)
    size = 128

    @pl.loop(0, half // size)
    def _(i):
        start = pl.multiple_of(i * size, size)
        forward_chunk(start, size, feat, weight, gain, scaled, slope, inv, pact)

    @pl.loop(0, d0 // 128)
    def _(i):
        start = pl.multiple_of(i * 128, 128)
        gw_ref[pl.ds(start, 128), :] = dot(pact[:, pl.ds(start, 128)], cot_ref[...], TN).astype(BF16)

    w = w_ref[...]

    @pl.loop(0, half // size)
    def _(i):
        start = pl.multiple_of(i * size, size)
        pooled = 0.5 * dot(pact[pl.ds(start, size), :], w, (((1,), (0,)), ((), ()))) + bias
        pooled_ref[pl.ds(start, size), :] = pooled.astype(BF16)

    @pl.loop(0, half // size)
    def _(i):
        start = pl.multiple_of(i * size, size)
        backward_chunk(start, size, cot_ref, w, gain, scaled, slope, inv, ge, gain_acc)

    chan, biases = small_grads(feat, ge, cot_ref, gain_acc, None)
    for d in range(dp):
        own = biases[d * part1 : (d + 1) * part1]
        small_ref[d, :part0, :] = own[:part0] + chan[d * part0 : (d + 1) * part0]
        small_ref[d, part0:, :] = own[part0:]


def shape(dims, kind):
    return jax.ShapeDtypeStruct(dims, kind)


def local(dp, seq, bases, embed_weight, embed_bias, norm_gain, proj_weight, proj_bias, cotangent):
    kernel_width, letters, part0 = embed_weight.shape
    part1 = proj_bias.shape[0]
    d0, d1 = part0 * dp, part1 * dp
    half = bases.shape[1] // 2
    codes = jnp.pad((bases[0] + 1).reshape(half, 2).T, ((0, 6), (0, 0)))
    lanes = jnp.pad(
        embed_weight.transpose(2, 1, 0), ((0, 0), (0, 0), (0, 16 - kernel_width))
    )
    lanes = lanes.at[:, 0, 15].set(embed_bias).reshape(part0, 64)
    packed = jnp.concatenate([lanes, norm_gain[:, None]], axis=1)
    packed = jnp.pad(packed, ((0, part1 - part0), (0, 63)))
    packed = packed.at[:, 65].set(proj_bias)
    up = [(i, i + 1) for i in range(seq - 1)]
    before = lax.ppermute(codes[:, half - 128 :], "seq", up)
    after = lax.ppermute(codes[:, :128], "seq", [(j, i) for i, j in up])
    halo = jnp.stack([before, after])
    packs = lax.all_gather(packed, "dp", axis=0)
    w = lax.all_gather(proj_weight, "dp", axis=0, tiled=True)
    vmem = pl.BlockSpec(memory_space=pltpu.VMEM)
    pooled, gw, small = pl.pallas_call(
        functools.partial(local_kernel, dp, kernel_width),
        out_shape=(shape((half, d1), BF16), shape((d0, d1), BF16), shape((dp, part1, 128), F32)),
        in_specs=[vmem] * 5,
        out_specs=(vmem,) * 3,
        scratch_shapes=[
            pltpu.VMEM((2, 16, half), jnp.int32),
            pltpu.VMEM((2, 64, half), BF16),
            pltpu.VMEM((2, half, d0), F32),
            pltpu.VMEM((2, half, d0), F32),
            pltpu.VMEM((2, half, 128), F32),
            pltpu.VMEM((half, d0), BF16),
            pltpu.VMEM((2, half, d0), BF16),
            pltpu.VMEM((8, d0), F32),
        ],
        compiler_params=pltpu.CompilerParams(vmem_limit_bytes=50 * 2**20),
        name="fused_step",
    )(codes, halo, packs, w, cotangent[0])
    gw = lax.psum(lax.psum_scatter(gw, "dp", scatter_dimension=0, tiled=True), "seq")
    small = lax.psum(lax.psum_scatter(small, "dp", scatter_dimension=0), "seq")
    return finish(pooled, gw, small, kernel_width, part0, half * seq * dp)


def finish(pooled, gw, small, kernel_width, part0, pairs):
    factor = 0.25 / pairs
    small = small * factor
    embed = small[:part0, :64].reshape(part0, 4, 16)
    return (
        pooled[None],
        embed[:, :, :kernel_width].transpose(2, 1, 0),
        embed[:, 0, 15],
        small[:part0, 64],
        gw.astype(F32) * factor,
        small[:, 65],
    )


def solution(mesh):
    placed = (
        P("dp", "seq"),
        P(None, None, "dp"),
        P("dp"),
        P("dp"),
        P("dp", None),
        P("dp"),
        P("dp", "seq", None),
    )
    return jax.shard_map(
        functools.partial(local, mesh.shape["dp"], mesh.shape["seq"]),
        mesh=mesh,
        in_specs=placed,
        out_specs=(
            P("dp", "seq", None),
            P(None, None, "dp"),
            P("dp"),
            P("dp"),
            P("dp", None),
            P("dp"),
        ),
        check_vma=False,
    )
```

```python
import functools

import jax
import jax.numpy as jnp
from jax import lax
from jax.experimental import pallas as pl
from jax.experimental.pallas import tpu as pltpu
from jax.sharding import PartitionSpec as P

F32, BF16 = jnp.float32, jnp.bfloat16
CUBIC = 0.044715
ROOT = 0.7978845608028654
NT = (((1,), (1,)), ((), ()))
TN = (((0,), (0,)), ((), ()))


def dot(a, b, dims):
    return lax.dot_general(a, b, dims, preferred_element_type=F32)


def build_features(codes_ref, halo_ref, stack_ref, feat_ref, kernel_width):
    half = codes_ref.shape[1]
    ext = jnp.concatenate([halo_ref[0], codes_ref[...], halo_ref[1]], axis=1)
    total = half + 256
    for parity in range(2):
        for k in range(kernel_width):
            source = parity + k - kernel_width // 2
            row, shift = source % 2, (source - source % 2) // 2
            moved = ext if shift == 0 else pltpu.roll(ext, (-shift) % total, 1)
            stack_ref[parity, k : k + 1, :] = moved[row : row + 1, 128 : 128 + half]
        stack_ref[parity, kernel_width : kernel_width + 1, :] = jnp.ones((1, half), jnp.int32)
        stack = stack_ref[parity]
        for c in range(4):
            feat_ref[parity, 16 * c : 16 * c + 16, :] = (
                jnp.where(stack == c + 1, 1.0, 0.0).astype(BF16)
            )


def pick_row(lane, packed):
    lanes = lax.broadcasted_iota(jnp.int32, (16, 128), 1)
    onehot = jnp.where(lanes == lane, 1.0, 0.0).astype(BF16)
    return dot(onehot, packed, NT)[0:1]


def forward_chunk(start, size, feat_ref, weight, gain, scaled_ref, slope_ref, inv_ref, pact_ref):
    total = None
    for parity in range(2):
        features = feat_ref[parity, :, pl.ds(start, size)]
        emb = dot(features, weight, (((0,), (1,)), ((), ())))
        emb = emb.astype(BF16).astype(F32)
        inverse = lax.rsqrt(jnp.mean(emb * emb, axis=1, keepdims=True) + 1e-6)
        scaled = emb * inverse
        x = scaled * gain
        sq = x * x
        t = jnp.tanh(x * (ROOT + (ROOT * CUBIC) * sq))
        half_x = 0.5 * x
        act = half_x + half_x * t
        half_t = 0.5 + 0.5 * t
        slope = half_t + half_x * (1.0 - t * t) * (ROOT + (3.0 * ROOT * CUBIC) * sq)
        scaled_ref[parity, pl.ds(start, size), :] = scaled
        slope_ref[parity, pl.ds(start, size), :] = slope
        inv_ref[parity, pl.ds(start, size), :] = jnp.broadcast_to(inverse, (size, 128))
        total = act if total is None else total + act
    pact_ref[pl.ds(start, size), :] = total.astype(BF16)


def backward_chunk(start, size, cot_ref, w, gain, scaled_ref, slope_ref, inv_ref, ge_ref, gain_acc):
    ga = dot(cot_ref[pl.ds(start, size), :], w, NT)
    width = ga.shape[1]
    for parity in range(2):
        scaled = scaled_ref[parity, pl.ds(start, size), :]
        inverse = inv_ref[parity, pl.ds(start, size), 0:1]
        u = ga * slope_ref[parity, pl.ds(start, size), :]
        q = u * scaled
        gain_acc[...] += jnp.sum(q.reshape(size // 8, 8, width), axis=0)
        mean = jnp.sum(q * gain, axis=1, keepdims=True) * (1.0 / width)
        ge = inverse * (u * gain - scaled * mean)
        ge_ref[parity, pl.ds(start, size), :] = ge.astype(BF16)


def small_grads(feat_ref, ge_ref, cot_ref, gain_acc):
    g = dot(feat_ref[0], ge_ref[0], (((1,), (0,)), ((), ())))
    g = g + dot(feat_ref[1], ge_ref[1], (((1,), (0,)), ((), ())))
    width = g.shape[1]
    gain_row = jnp.sum(gain_acc[...], axis=0, keepdims=True)
    rows = lax.broadcasted_iota(jnp.int32, (64, width), 0)
    g = jnp.where(rows == 31, gain_row, g)
    channels = jnp.concatenate([g, jnp.zeros_like(g)], axis=0).T
    ones = jnp.ones((16, cot_ref.shape[0]), BF16)
    pb = 2.0 * dot(ones, cot_ref[...], (((1,), (0,)), ((), ())))[0:1]
    rows = lax.broadcasted_iota(jnp.int32, (128, pb.shape[1]), 0)
    biases = jnp.where(rows == 64, pb, 0.0).T
    return channels, biases


def local_kernel(dp, kernel_width, codes_ref, halo_ref, packed_ref, w_ref, cot_ref,
                 pooled_ref, gw_ref, small_ref,
                 stack, feat, scaled, slope, inv, pact, ge, gain_acc):
    half = codes_ref.shape[1]
    d0, d1 = w_ref.shape
    part0, part1 = d0 // dp, d1 // dp
    build_features(codes_ref, halo_ref, stack, feat, kernel_width)
    channels = jnp.concatenate([packed_ref[d, :part0, :] for d in range(dp)], axis=0)
    weight = channels[:, :64]
    gain = pick_row(31, channels)
    bias = pick_row(64, jnp.concatenate([packed_ref[d] for d in range(dp)], axis=0))
    gain_acc[...] = jnp.zeros_like(gain_acc)
    size = 128

    @pl.loop(0, half // size)
    def _(i):
        start = pl.multiple_of(i * size, size)
        forward_chunk(start, size, feat, weight, gain, scaled, slope, inv, pact)

    @pl.loop(0, d0 // 128)
    def _(i):
        start = pl.multiple_of(i * 128, 128)
        gw_ref[pl.ds(start, 128), :] = dot(pact[:, pl.ds(start, 128)], cot_ref[...], TN).astype(BF16)

    w = w_ref[...]

    @pl.loop(0, half // size)
    def _(i):
        start = pl.multiple_of(i * size, size)
        pooled = 0.5 * dot(pact[pl.ds(start, size), :], w, (((1,), (0,)), ((), ()))) + bias
        pooled_ref[pl.ds(start, size), :] = pooled.astype(BF16)

    @pl.loop(0, half // size)
    def _(i):
        start = pl.multiple_of(i * size, size)
        backward_chunk(start, size, cot_ref, w, gain, scaled, slope, inv, ge, gain_acc)

    chan, biases = small_grads(feat, ge, cot_ref, gain_acc)
    for d in range(dp):
        own = biases[d * part1 : (d + 1) * part1]
        small_ref[d, :part0, :] = own[:part0] + chan[d * part0 : (d + 1) * part0]
        small_ref[d, part0:, :] = own[part0:]


MESH = pl.DeviceIdType.MESH


def fused_kernel(kernel_width, codes_ref, rows_ref, w_ref, cot_hbm,
                 pooled_hbm, gw_ref, small_out,
                 halo, stack, feat, scaled, slope, inv, pact, ge, gain_acc,
                 pack, packs, wbuf, cot, pooled, gwb, s1buf, p1, s2buf, sum2, s3buf, fin,
                 small, sbuf, tbuf,
                 send_sem, halo_recv, pack_recv, w_recv, s1_recv, s2_recv, s3_recv, fin_recv,
                 small_recv, t_recv, local_sem):
    dp, seq = 8, 4
    half = codes_ref.shape[1]
    part0, d1 = w_ref.shape
    d0, part1, part_h = part0 * dp, d1 // dp, part0 // 2
    me, pos = lax.axis_index("dp"), lax.axis_index("seq")
    z, y, x, c = me // 2, me % 2, pos // 2, pos % 2
    y2, x2, c2 = 1 - y, 1 - x, 1 - c
    own_rank = z % 2 == x
    factor = 0.25 / (half * seq * dp)

    cot_in = pltpu.make_async_copy(cot_hbm, cot, local_sem.at[0])
    cot_in.start()

    pack[...] = rows_ref[...].T[:part1].astype(BF16)
    packs[me] = pack[...]
    wbuf[me] = w_ref[...].reshape(2, part_h, d1)

    barrier = pltpu.get_barrier_semaphore()
    for j in range(1, dp):
        pl.semaphore_signal(
            barrier, inc=1, device_id={"dp": (me + j) % dp, "seq": pos}, device_id_type=MESH
        )
    for j in range(1, seq):
        pl.semaphore_signal(
            barrier, inc=1, device_id={"dp": me, "seq": (pos + j) % seq}, device_id_type=MESH
        )
        pl.semaphore_signal(
            barrier,
            inc=1,
            device_id={"dp": 2 * z + y2, "seq": (pos + j) % seq},
            device_id_type=MESH,
        )
    pl.semaphore_wait(barrier, dp - 1 + 2 * (seq - 1))

    started = []

    def send(src, dst, recv, to_dp, to_seq, pred=None):
        copy = pltpu.make_async_remote_copy(
            src_ref=src, dst_ref=dst, send_sem=send_sem.at[len(started)], recv_sem=recv,
            device_id={"dp": to_dp, "seq": to_seq}, device_id_type=MESH,
        )
        started.append((copy, pred))
        if pred is None:
            copy.start()
        else:
            pl.when(pred)(lambda: copy.start())

    def arrive(dst, recv, pred=None):
        copy = pltpu.make_async_remote_copy(
            src_ref=dst, dst_ref=dst, send_sem=send_sem.at[0], recv_sem=recv,
            device_id={"dp": me, "seq": (pos + 1) % seq}, device_id_type=MESH,
        )
        if pred is None:
            copy.wait_recv()
        else:
            pl.when(pred)(lambda: copy.wait_recv())

    for j in range(1, dp):
        send(pack, packs.at[me], pack_recv.at[me], (me + j) % dp, pos)
    send(codes_ref.at[:, half - 128 :], halo.at[0], halo_recv.at[0], me, pos + 1, pos < seq - 1)
    send(codes_ref.at[:, :128], halo.at[1], halo_recv.at[1], me, pos - 1, pos > 0)
    for zz in range(4):
        send(wbuf.at[me, c], wbuf.at[me, c], w_recv.at[me, c], 2 * zz + y, pos,
             own_rank & (z != zz))
    send(wbuf.at[me, c], wbuf.at[me, c], w_recv.at[me, c], 2 * z + y2, pos)

    gain_acc[...] = jnp.zeros_like(gain_acc)
    arrive(halo.at[0], halo_recv.at[0], pos > 0)
    arrive(halo.at[1], halo_recv.at[1], pos < seq - 1)

    @pl.when(pos == 0)
    def _():
        halo[0] = jnp.zeros(halo.shape[1:], jnp.int32)

    @pl.when(pos == seq - 1)
    def _():
        halo[1] = jnp.zeros(halo.shape[1:], jnp.int32)

    build_features(codes_ref, halo, stack, feat, kernel_width)
    for j in range(1, dp):
        arrive(packs.at[(me + j) % dp], pack_recv.at[(me + j) % dp])
    channels = jnp.concatenate([packs[d, :part0, :] for d in range(dp)], axis=0)
    weight = channels[:, :64]
    gain = pick_row(31, channels)
    bias = pick_row(64, packs[...].reshape(dp * part1, 128))
    size = 128
    chunks = half // size

    def forward(first, last):
        @pl.loop(first, last)
        def _(i):
            start = pl.multiple_of(i * size, size)
            forward_chunk(start, size, feat, weight, gain, scaled, slope, inv, pact)

    forward(0, chunks // 3)
    for zz in range(4):
        d = 2 * zz + y
        slot, sem = wbuf.at[d, c], w_recv.at[d, c]
        other = z != zz
        direct = other & (x == zz % 2)
        arrive(slot, sem, direct)
        send(slot, slot, sem, 2 * z + y2, pos, direct)
        send(slot, slot, sem, me, 2 * x2 + c, direct)
        send(slot, slot, sem, 2 * z + y2, 2 * x2 + c, direct)
        send(slot, slot, sem, me, 2 * x + c2, direct)
    d = 2 * z + y2
    arrive(wbuf.at[d, c], w_recv.at[d, c])
    send(wbuf.at[d, c], wbuf.at[d, c], w_recv.at[d, c], me, 2 * x + c2)
    forward(chunks // 3, chunks)
    for zz in range(4):
        d = 2 * zz + y
        slot, sem = wbuf.at[d, c], w_recv.at[d, c]
        relayed = (z != zz) & (x != zz % 2)
        arrive(slot, sem, relayed)
        send(slot, slot, sem, me, 2 * x + c2, relayed)
        d = 2 * zz + y2
        slot, sem = wbuf.at[d, c], w_recv.at[d, c]
        arrive(slot, sem, z != zz)
        send(slot, slot, sem, me, 2 * x + c2, z != zz)

    cot_in.wait()
    block = d0 // 2
    for b in range(2):
        value = dot(pact[:, b * block : (b + 1) * block], cot[...], TN)
        gwb[4 * b : 4 * b + 4] = value.astype(BF16).reshape(4, 2, part_h, d1)
        send(gwb.at[4 * b : 4 * b + 4, c2], s1buf.at[b], s1_recv.at[b], me, 2 * x + c2)

    for d in range(dp):
        arrive(wbuf.at[d, c2], w_recv.at[d, c2], me != d)

    @pl.loop(0, chunks)
    def _(i):
        start = pl.multiple_of(i * size, size)
        w = wbuf[...].reshape(d0, d1)
        value = 0.5 * dot(pact[pl.ds(start, size), :], w, (((1,), (0,)), ((), ()))) + bias
        pooled[pl.ds(start, size), :] = value.astype(BF16)

    pooled_out = pltpu.make_async_copy(pooled, pooled_hbm, local_sem.at[1])
    pooled_out.start()

    for b in range(2):
        arrive(s1buf.at[b], s1_recv.at[b])
        for k in range(4):
            p1[b, k] = (gwb[4 * b + k, c].astype(F32) + s1buf[b, k].astype(F32)).astype(BF16)
    rank = 2 * x + y
    send(p1.at[:, 2 * x + y2], s2buf.at[rank], s2_recv.at[rank], 2 * z + y2, pos)
    send(p1.at[:, 2 * x2 + y], s2buf.at[rank], s2_recv.at[rank], me, 2 * x2 + c)
    send(p1.at[:, 2 * x2 + y2], s2buf.at[rank], s2_recv.at[rank], 2 * z + y2, 2 * x2 + c)

    def backward(first, last):
        @pl.loop(first, last)
        def _(i):
            start = pl.multiple_of(i * size, size)
            w = wbuf[...].reshape(d0, d1)
            backward_chunk(start, size, cot, w, gain, scaled, slope, inv, ge, gain_acc)

    backward(0, chunks // 2)
    total = [p1[k, rank].astype(F32) for k in range(2)]
    for other in (2 * x + y2, 2 * x2 + y, 2 * x2 + y2):
        arrive(s2buf.at[other], s2_recv.at[other])
        total = [total[k] + s2buf[other, k].astype(F32) for k in range(2)]
    for k in range(2):
        sum2[k] = total[k].astype(BF16)
    for k in range(2):
        zt = x + 2 * k
        send(sum2.at[k], s3buf.at[z], s3_recv.at[z], 2 * zt + y, pos, zt != z)
    backward(chunks // 2, chunks)

    chan, biases = small_grads(feat, ge, cot, gain_acc)
    for d in range(dp):
        own = biases[d * part1 : (d + 1) * part1]
        small[d, :part0, :] = (own[:part0] + chan[d * part0 : (d + 1) * part0]).astype(BF16)
        small[d, part0:, :] = own[part0:].astype(BF16)
    for j in range(1, dp):
        to = (me + j) % dp
        send(small.at[to], sbuf.at[me], small_recv.at[me], to, pos)

    for zz in range(4):
        arrive(s3buf.at[zz], s3_recv.at[zz], own_rank & (z != zz))

    @pl.when(own_rank)
    def _():
        value = sum2[z // 2].astype(F32)
        for j in range(1, 4):
            value = value + s3buf[(z + j) % 4].astype(F32)
        fin[c] = value.astype(BF16)

    for to in (2 * x + c2, 2 * x2 + c, 2 * x2 + c2):
        send(fin.at[c], fin.at[c], fin_recv.at[c], me, to, own_rank)

    sbuf[me] = small[me]
    for j in range(1, dp):
        arrive(sbuf.at[(me + j) % dp], small_recv.at[(me + j) % dp])
    tbuf[pos] = jnp.sum(sbuf[...].astype(F32), axis=0).astype(BF16)
    for j in range(1, seq):
        send(tbuf.at[pos], tbuf.at[pos], t_recv.at[pos], me, (pos + j) % seq)

    arrive(fin.at[c2], fin_recv.at[c2])
    arrive(fin.at[c], fin_recv.at[c], jnp.logical_not(own_rank))
    gw_ref[...] = fin[...].astype(F32).reshape(part0, d1) * factor
    for j in range(1, seq):
        arrive(tbuf.at[(pos + j) % seq], t_recv.at[(pos + j) % seq])
    value = jnp.sum(tbuf[...].astype(F32), axis=0) * factor
    padded = jnp.concatenate([value, jnp.zeros((128 - part1, 128), F32)], axis=0)
    small_out[...] = padded.T

    for copy, pred in started:
        if pred is None:
            copy.wait_send()
        else:
            pl.when(pred)(lambda copy=copy: copy.wait_send())
    pooled_out.wait()


def shape(dims, kind):
    return jax.ShapeDtypeStruct(dims, kind)


def fused(kernel_width, codes, rows, proj_weight, cot):
    half = codes.shape[1]
    part0, d1 = proj_weight.shape
    dp, seq = 8, 4
    d0, part1, part_h = part0 * dp, d1 // dp, part0 // 2
    vmem, hbm = pl.BlockSpec(memory_space=pltpu.VMEM), pl.BlockSpec(memory_space=pl.ANY)
    dma = pltpu.SemaphoreType.DMA
    return pl.pallas_call(
        functools.partial(fused_kernel, kernel_width),
        out_shape=(shape((half, d1), BF16), shape((part0, d1), F32), shape((128, 128), F32)),
        in_specs=[vmem, vmem, vmem, hbm],
        out_specs=(hbm, vmem, vmem),
        scratch_shapes=[
            pltpu.VMEM((2, 8, 128), jnp.int32),
            pltpu.VMEM((2, 16, half), jnp.int32),
            pltpu.VMEM((2, 64, half), BF16),
            pltpu.VMEM((2, half, d0), F32),
            pltpu.VMEM((2, half, d0), F32),
            pltpu.VMEM((2, half, 128), F32),
            pltpu.VMEM((half, d0), BF16),
            pltpu.VMEM((2, half, d0), BF16),
            pltpu.VMEM((8, d0), F32),
            pltpu.VMEM((part1, 128), BF16),
            pltpu.VMEM((dp, part1, 128), BF16),
            pltpu.VMEM((dp, 2, part_h, d1), BF16),
            pltpu.VMEM((half, d1), BF16),
            pltpu.VMEM((half, d1), BF16),
            pltpu.VMEM((dp, 2, part_h, d1), BF16),
            pltpu.VMEM((2, 4, part_h, d1), BF16),
            pltpu.VMEM((2, 4, part_h, d1), BF16),
            pltpu.VMEM((4, 2, part_h, d1), BF16),
            pltpu.VMEM((2, part_h, d1), BF16),
            pltpu.VMEM((4, part_h, d1), BF16),
            pltpu.VMEM((2, part_h, d1), BF16),
            pltpu.VMEM((dp, part1, 128), BF16),
            pltpu.VMEM((dp, part1, 128), BF16),
            pltpu.VMEM((seq, part1, 128), BF16),
            dma((72,)),
            dma((2,)),
            dma((dp,)),
            dma((dp, 2)),
            dma((2,)),
            dma((4,)),
            dma((4,)),
            dma((2,)),
            dma((dp,)),
            dma((seq,)),
            dma((2,)),
        ],
        compiler_params=pltpu.CompilerParams(
            collective_id=0, has_side_effects=True, vmem_limit_bytes=50 * 2**20
        ),
        name="fused_step",
    )(codes, rows, proj_weight, cot)


def local(dp, seq, bases, embed_weight, embed_bias, norm_gain, proj_weight, proj_bias, cotangent):
    kernel_width, letters, part0 = embed_weight.shape
    part1 = proj_bias.shape[0]
    d0, d1 = part0 * dp, part1 * dp
    half = bases.shape[1] // 2
    codes = jnp.pad((bases[0] + 1).reshape(half, 2).T, ((0, 6), (0, 0)))
    spare = jnp.stack([embed_bias, norm_gain, jnp.zeros_like(norm_gain), jnp.zeros_like(norm_gain)])
    spare = jnp.pad(spare[:, None], ((0, 0), (0, 16 - kernel_width - 1), (0, 0)))
    rows = jnp.concatenate([embed_weight.transpose(1, 0, 2), spare], axis=1).reshape(64, part0)
    rows = jnp.pad(rows, ((0, 0), (0, 128 - part0)))
    rows = jnp.concatenate([rows, jnp.pad(proj_bias, (0, 128 - part1))[None]], axis=0)
    rows = jnp.pad(rows.astype(F32), ((0, 63), (0, 0)))
    if (dp, seq) == (8, 4) and part0 % 32 == 0:
        pooled, gw, small = fused(kernel_width, codes, rows, proj_weight, cotangent[0])
    else:
        pooled, gw, small = separate(dp, seq, kernel_width, codes, rows, proj_weight, cotangent[0])
    embed = small[:64, :part0].reshape(4, 16, part0)
    return (
        pooled[None],
        embed[:, :kernel_width].transpose(1, 0, 2),
        small[15, :part0],
        small[31, :part0],
        gw,
        small[64, :part1],
    )


def separate(dp, seq, kernel_width, codes, rows, proj_weight, cot):
    half = codes.shape[1]
    part0, d1 = proj_weight.shape
    d0, part1 = part0 * dp, d1 // dp
    up = [(i, i + 1) for i in range(seq - 1)]
    before = lax.ppermute(codes[:, half - 128 :], "seq", up)
    after = lax.ppermute(codes[:, :128], "seq", [(j, i) for i, j in up])
    halo = jnp.stack([before, after])
    packs = lax.all_gather(rows.T[:part1].astype(BF16), "dp", axis=0)
    w = lax.all_gather(proj_weight, "dp", axis=0, tiled=True)
    vmem = pl.BlockSpec(memory_space=pltpu.VMEM)
    pooled, gw, small = pl.pallas_call(
        functools.partial(local_kernel, dp, kernel_width),
        out_shape=(shape((half, d1), BF16), shape((d0, d1), BF16), shape((dp, part1, 128), F32)),
        in_specs=[vmem] * 5,
        out_specs=(vmem,) * 3,
        scratch_shapes=[
            pltpu.VMEM((2, 16, half), jnp.int32),
            pltpu.VMEM((2, 64, half), BF16),
            pltpu.VMEM((2, half, d0), F32),
            pltpu.VMEM((2, half, d0), F32),
            pltpu.VMEM((2, half, 128), F32),
            pltpu.VMEM((half, d0), BF16),
            pltpu.VMEM((2, half, d0), BF16),
            pltpu.VMEM((8, d0), F32),
        ],
        compiler_params=pltpu.CompilerParams(vmem_limit_bytes=50 * 2**20),
        name="local_step",
    )(codes, halo, packs, w, cot)
    gw = lax.psum(lax.psum_scatter(gw, "dp", scatter_dimension=0, tiled=True), "seq")
    small = lax.psum(lax.psum_scatter(small, "dp", scatter_dimension=0), "seq")
    factor = 0.25 / (half * seq * dp)
    small = jnp.pad(small.T * factor, ((0, 0), (0, 128 - part1)))
    return pooled, gw.astype(F32) * factor, small


def solution(mesh):
    placed = (
        P("dp", "seq"),
        P(None, None, "dp"),
        P("dp"),
        P("dp"),
        P("dp", None),
        P("dp"),
        P("dp", "seq", None),
    )
    return jax.shard_map(
        functools.partial(local, mesh.shape["dp"], mesh.shape["seq"]),
        mesh=mesh,
        in_specs=placed,
        out_specs=(
            P("dp", "seq", None),
            P(None, None, "dp"),
            P("dp"),
            P("dp"),
            P("dp", None),
            P("dp"),
        ),
        check_vma=False,
    )
```

```python
import functools

import jax
import jax.numpy as jnp
from jax import lax
from jax.experimental import pallas as pl
from jax.experimental.pallas import tpu as pltpu
from jax.sharding import PartitionSpec as P

F32, BF16 = jnp.float32, jnp.bfloat16
CUBIC = 0.044715
ROOT = 0.7978845608028654
NN = (((1,), (0,)), ((), ()))
NT = (((1,), (1,)), ((), ()))
TN = (((0,), (0,)), ((), ()))
MESH = pl.DeviceIdType.MESH
STEP = 16


def dot(a, b, dims):
    return lax.dot_general(a, b, dims, preferred_element_type=F32)


def build_features(bases_ref, halo_ref, stack_ref, wide_ref, feat_ref, kernel_width):
    length = bases_ref.shape[1]
    half, total = length // 2, length + 256
    ext = jnp.concatenate([halo_ref[0:1], bases_ref[...] + 1, halo_ref[1:2]], axis=1)
    ext = jnp.broadcast_to(ext, (8, total))
    for k in range(kernel_width):
        shift = k - kernel_width // 2
        moved = ext if shift == 0 else pltpu.roll(ext, (-shift) % total, 1)
        stack_ref[k : k + 1, :] = moved[0:1, 128 : 128 + length]
    stack_ref[kernel_width : kernel_width + 1, :] = jnp.ones((1, length), jnp.int32)
    stack = stack_ref[...]
    hot = jnp.concatenate([jnp.where(stack == c + 1, 1.0, 0.0) for c in range(4)] * 2, axis=0)
    wide_ref[...] = hot.T
    for parity in range(2):
        feat_ref[parity] = wide_ref[pl.ds(parity, half, stride=2), :][:, :64].astype(BF16)


def forward_chunk(start, size, feat_ref, weight, gain, emb_ref, scaled_ref, slope_ref, inv_ref, pact_ref):
    for parity in range(2):
        emb_ref[parity] = dot(feat_ref[parity, pl.ds(start, size), :], weight, NT)
    for r in range(0, size, STEP):
        rows = pl.ds(start + r, STEP)
        total = None
        for parity in range(2):
            emb = emb_ref[parity, r : r + STEP, :].astype(BF16).astype(F32)
            inverse = lax.rsqrt(jnp.mean(emb * emb, axis=1, keepdims=True) + 1e-6)
            scaled = emb * inverse
            x = scaled * gain
            sq = x * x
            t = 0.5 + 0.5 * jnp.tanh(x * (ROOT + (ROOT * CUBIC) * sq))
            act = x * t
            slope = t + act * (1.0 - t) * (2.0 * ROOT + (6.0 * ROOT * CUBIC) * sq)
            scaled_ref[parity, rows, :] = scaled
            slope_ref[parity, rows, :] = slope
            inv_ref[parity, rows, :] = jnp.broadcast_to(inverse, (STEP, 128))
            total = act if total is None else total + act
        pact_ref[rows, :] = total.astype(BF16)


def backward_chunk(start, size, cot_ref, w, gain, ga_ref, scaled_ref, slope_ref, inv_ref, ge_ref, acc_ref):
    ga_ref[...] = dot(cot_ref[start : start + size, :], w, NT)
    width = ga_ref.shape[1]
    acc = acc_ref[...]
    for r in range(0, size, STEP):
        rows = slice(start + r, start + r + STEP)
        ga = ga_ref[r : r + STEP, :]
        for parity in range(2):
            scaled = scaled_ref[parity, rows, :]
            inverse = inv_ref[parity, rows, 0:1]
            u = ga * slope_ref[parity, rows, :]
            q = u * scaled
            acc = acc + (q[:8] + q[8:])
            mean = jnp.sum(q * gain, axis=1, keepdims=True) * (1.0 / width)
            ge = inverse * (u * gain - scaled * mean)
            ge_ref[parity, rows, :] = ge.astype(BF16)
    acc_ref[...] = acc


def fused_kernel(
    kernel_width,
    bases_hbm, ew_hbm, eb_hbm, gain_hbm, w_hbm, pb_hbm, cot_hbm,
    pooled_hbm, gw_ref, small_out,
    pooled, bases, ew, eb, gain_in, pb, halo, stack, wide, feat, emb, scaled, slope, inv, pact, ge, ga, acc,
    rows_in, pack, packs, wbuf, cot, gwb, s1buf, p1, s2buf, sum2, s3buf, fin, small, sbuf, tbuf,
    send_sem, halo_recv, pack_recv, w_recv, s1_recv, s2_recv, s3_recv, fin_recv,
    small_recv, t_recv, local_sem,
):
    dp, seq = 8, 4
    length = bases.shape[1]
    half = length // 2
    part0, d1 = w_hbm.shape
    d0, part1, part_h = part0 * dp, d1 // dp, part0 // 2
    me, pos = lax.axis_index("dp"), lax.axis_index("seq")
    z, y, x, c = me // 2, me % 2, pos // 2, pos % 2
    y2, x2, c2 = 1 - y, 1 - x, 1 - c
    mate, across, skew = 2 * x + c2, 2 * x2 + c, 2 * x2 + c2
    own_rank = z % 2 == x
    factor = 0.25 / (half * seq * dp)

    barrier = pltpu.get_barrier_semaphore()
    for j in range(1, dp):
        pl.semaphore_signal(
            barrier, inc=1, device_id={"dp": (me + j) % dp, "seq": pos}, device_id_type=MESH
        )
    for j in range(1, seq):
        for to in (me, 2 * z + y2):
            pl.semaphore_signal(
                barrier, inc=1, device_id={"dp": to, "seq": (pos + j) % seq}, device_id_type=MESH
            )

    loads = [
        pltpu.make_async_copy(src, dst, local_sem.at[i])
        for i, (src, dst) in enumerate(
            [
                (ew_hbm, ew), (eb_hbm, eb), (gain_hbm, gain_in), (pb_hbm, pb), (bases_hbm, bases),
                (w_hbm.at[:part_h], wbuf.at[me, 0]), (w_hbm.at[part_h:], wbuf.at[me, 1]),
                (cot_hbm, cot),
            ]
        )
    ]
    for load in loads:
        load.start()
    rows_in[...] = jnp.zeros_like(rows_in)
    acc[...] = jnp.zeros_like(acc)
    for load in loads[:4]:
        load.wait()
    values = ew[...].astype(F32)
    for letter in range(4):
        rows_in[16 * letter : 16 * letter + kernel_width, :part0] = values[:, letter, :]
    rows_in[15:16, :part0] = eb[...].astype(F32)
    rows_in[31:32, :part0] = gain_in[...].astype(F32)
    turned = rows_in[...].T
    pack[:part_h, :] = jnp.concatenate(
        [turned[:part_h, :64], turned[part_h:part0, :64]], axis=1
    ).astype(BF16)
    tail = jnp.concatenate([pb[...].astype(F32), jnp.zeros((1, 128 - part1), F32)], axis=1)
    pack[part_h:, :] = jnp.broadcast_to(tail, (16, 128)).astype(BF16)
    packs[me] = pack[...]
    for load in loads[4:7]:
        load.wait()

    pl.semaphore_wait(barrier, dp - 1 + 2 * (seq - 1))

    started = []

    def send(src, dst, recv, to_dp, to_seq, pred=None):
        copy = pltpu.make_async_remote_copy(
            src_ref=src, dst_ref=dst, send_sem=send_sem.at[len(started)], recv_sem=recv,
            device_id={"dp": to_dp, "seq": to_seq}, device_id_type=MESH,
        )
        started.append((copy, pred))
        if pred is None:
            copy.start()
        else:
            pl.when(pred)(lambda: copy.start())

    def arrive(dst, recv, pred=None):
        copy = pltpu.make_async_remote_copy(
            src_ref=dst, dst_ref=dst, send_sem=send_sem.at[0], recv_sem=recv,
            device_id={"dp": me, "seq": mate}, device_id_type=MESH,
        )
        if pred is None:
            copy.wait_recv()
        else:
            pl.when(pred)(lambda: copy.wait_recv())

    send(bases.at[:, length - 128 :], halo.at[0:1], halo_recv.at[0], me, pos + 1, pos < seq - 1)
    send(bases.at[:, :128], halo.at[1:2], halo_recv.at[1], me, pos - 1, pos > 0)
    for j in range(1, dp):
        send(pack, packs.at[me], pack_recv.at[me], (me + j) % dp, pos)
    for zz in range(4):
        send(wbuf.at[me, c], wbuf.at[me, c], w_recv.at[me, c], 2 * zz + y, pos,
             own_rank & (z != zz))
    send(wbuf.at[me, c], wbuf.at[me, c], w_recv.at[me, c], 2 * z + y2, pos)

    arrive(halo.at[0:1], halo_recv.at[0], pos > 0)
    arrive(halo.at[1:2], halo_recv.at[1], pos < seq - 1)
    for side, edge in ((0, 0), (1, seq - 1)):

        @pl.when(pos == edge)
        def _(side=side):
            halo[side : side + 1, :] = jnp.zeros((1, 128), jnp.int32)

        @pl.when(pos != edge)
        def _(side=side):
            halo[side : side + 1, :] = halo[side : side + 1, :] + 1


    build_features(bases, halo, stack, wide, feat, kernel_width)
    for j in range(1, dp):
        arrive(packs.at[(me + j) % dp], pack_recv.at[(me + j) % dp])
    weight = jnp.concatenate(
        [packs[d, :part_h, 64 * h : 64 * h + 64] for d in range(dp) for h in range(2)], axis=0
    )
    lanes = lax.broadcasted_iota(jnp.int32, (16, 64), 1)
    gain = dot(jnp.where(lanes == 31, 1.0, 0.0).astype(BF16), weight, NT)[0:1]
    size = 128
    chunks = half // size

    def forward(first, last):
        @pl.loop(first, last)
        def _(i):
            start = pl.multiple_of(i * size, size)
            forward_chunk(start, size, feat, weight, gain, emb, scaled, slope, inv, pact)

    forward(0, chunks // 3)
    for zz in range(4):
        d = 2 * zz + y
        slot, sem = wbuf.at[d, c], w_recv.at[d, c]
        direct = (z != zz) & (x == zz % 2)
        arrive(slot, sem, direct)
        send(slot, slot, sem, 2 * z + y2, across, direct)
        send(slot, slot, sem, 2 * z + y2, pos, direct)
        send(slot, slot, sem, me, across, direct)
        send(slot, slot, sem, me, mate, direct)
    d = 2 * z + y2
    arrive(wbuf.at[d, c], w_recv.at[d, c])
    send(wbuf.at[d, c], wbuf.at[d, c], w_recv.at[d, c], me, mate)
    forward(chunks // 3, chunks)

    loads[7].wait()
    block = d0 // 2
    for b in range(2):
        value = dot(pact[:, b * block : (b + 1) * block], cot[...], TN)
        gwb[4 * b : 4 * b + 4] = value.astype(BF16).reshape(4, 2, part_h, d1)
        send(gwb.at[4 * b : 4 * b + 4, c2], s1buf.at[b], s1_recv.at[b], me, mate)

    for zz in range(4):
        d = 2 * zz + y
        slot, sem = wbuf.at[d, c], w_recv.at[d, c]
        relayed = (z != zz) & (x != zz % 2)
        arrive(slot, sem, relayed)
        send(slot, slot, sem, me, mate, relayed)
        d = 2 * zz + y2
        slot, sem = wbuf.at[d, c], w_recv.at[d, c]
        arrive(slot, sem, z != zz)
        send(slot, slot, sem, me, mate, z != zz)

    rank = 2 * x + y
    others = (
        (2 * x2 + y2, 2 * z + y2, across),
        (2 * x + y2, 2 * z + y2, pos),
        (2 * x2 + y, me, across),
    )
    for b in range(2):
        arrive(s1buf.at[b], s1_recv.at[b])
        for k in range(4):
            p1[b, k] = (gwb[4 * b + k, c].astype(F32) + s1buf[b, k].astype(F32)).astype(BF16)
        for piece, to_dp, to_seq in others:
            send(p1.at[b, piece], s2buf.at[b, rank], s2_recv.at[b, rank], to_dp, to_seq)

    for d in range(dp):
        arrive(wbuf.at[d, c2], w_recv.at[d, c2], me != d)

    tails = jnp.concatenate([packs[d, part_h:, :][0:1].astype(F32) for d in range(dp)], axis=0)
    tails = jnp.concatenate([tails, jnp.zeros((8, 128), F32)], axis=0).astype(BF16)
    columns = lax.broadcasted_iota(jnp.int32, (128, d1), 1)
    lane = lax.broadcasted_iota(jnp.int32, (128, d1), 0)
    place = jnp.where((columns % part1) == lane, 1.0, 0.0).astype(BF16)
    spread = dot(tails, place, NN)
    holder = lax.broadcasted_iota(jnp.int32, (16, d1), 0)
    column = lax.broadcasted_iota(jnp.int32, (16, d1), 1)
    bias = jnp.sum(jnp.where(column // part1 == holder, spread, 0.0), axis=0, keepdims=True)

    big = half // 3
    for i in range(3):
        w = wbuf[...].reshape(d0, d1)
        value = 0.5 * dot(pact[i * big : (i + 1) * big, :], w, NN) + bias
        pooled[i * big : (i + 1) * big, :] = value.astype(BF16)
    pooled_out = pltpu.make_async_copy(pooled, pooled_hbm, local_sem.at[8])
    pooled_out.start()

    def backward(i):
        w = wbuf[...].reshape(d0, d1)
        backward_chunk(i * big, big, cot, w, gain, ga.at[i % 2], scaled, slope, inv, ge, acc)

    def plane_sum(k):
        total = p1[k, rank].astype(F32)
        for piece, _, _ in others:
            arrive(s2buf.at[k, piece], s2_recv.at[k, piece])
            total = total + s2buf[k, piece].astype(F32)
        sum2[k] = total.astype(BF16)
        zt = x + 2 * k
        send(sum2.at[k], s3buf.at[z], s3_recv.at[z], 2 * zt + y, pos, zt != z)

    backward(0)
    plane_sum(0)
    backward(1)
    plane_sum(1)
    backward(2)

    g = dot(feat[0], ge[0], TN) + dot(feat[1], ge[1], TN)
    gain_row = jnp.sum(acc[...], axis=0, keepdims=True)
    g = jnp.where(lax.broadcasted_iota(jnp.int32, (64, d0), 0) == 31, gain_row, g)
    turned = jnp.concatenate([g, jnp.zeros_like(g)], axis=0).T
    for d in range(dp):
        low = turned[d * part0 : d * part0 + part_h, :64]
        high = turned[d * part0 + part_h : (d + 1) * part0, :64]
        small[d, :part_h, :] = jnp.concatenate([low, high], axis=1).astype(BF16)
    sums = 2.0 * dot(jnp.ones((16, half), BF16), cot[...], NN)[0:8]
    for d in range(dp):
        own = jnp.concatenate(
            [sums[:, d * part1 : (d + 1) * part1], jnp.zeros((8, 128 - part1), F32)], axis=1
        )
        small[d, part_h:, :] = jnp.concatenate([own, own], axis=0).astype(BF16)
    for j in range(1, dp):
        to = (me + j) % dp
        send(small.at[to], sbuf.at[me], small_recv.at[me], to, pos)
    sbuf[me] = small[me]

    for zz in range(4):
        arrive(s3buf.at[zz], s3_recv.at[zz], own_rank & (z != zz))

    @pl.when(own_rank)
    def _():
        value = sum2[z // 2].astype(F32)
        for j in range(1, 4):
            value = value + s3buf[(z + j) % 4].astype(F32)
        fin[c] = value.astype(BF16)

    send(fin.at[c], fin.at[c], fin_recv.at[c], me, across, own_rank)
    arrive(fin.at[c], fin_recv.at[c], jnp.logical_not(own_rank))
    send(fin.at[c], fin.at[c], fin_recv.at[c], me, mate)

    for j in range(1, dp):
        arrive(sbuf.at[(me + j) % dp], small_recv.at[(me + j) % dp])
    tbuf[pos] = jnp.sum(sbuf[...].astype(F32), axis=0).astype(BF16)
    for j in range(1, seq):
        send(tbuf.at[pos], tbuf.at[pos], t_recv.at[pos], me, (pos + j) % seq)

    arrive(fin.at[c2], fin_recv.at[c2])
    gw_ref[...] = fin[...].astype(F32).reshape(part0, d1) * factor
    for j in range(1, seq):
        arrive(tbuf.at[(pos + j) % seq], t_recv.at[(pos + j) % seq])
    small_out[...] = jnp.sum(tbuf[...].astype(F32), axis=0) * factor

    for copy, pred in started:
        if pred is None:
            copy.wait_send()
        else:
            pl.when(pred)(lambda copy=copy: copy.wait_send())
    pooled_out.wait()


def finish_kernel(kernel_width, pooled_in, gw_in, small, pooled, gew, geb, ggain, gw, gpb, turned, sems):
    part0, part1 = gw_in.shape[0], gpb.shape[1]
    part_h = part0 // 2
    copies = [
        pltpu.make_async_copy(pooled_in, pooled, sems.at[0]),
        pltpu.make_async_copy(gw_in, gw, sems.at[1]),
    ]
    for copy in copies:
        copy.start()
    gpb[...] = small[part_h : part_h + 1, :part1]
    low, high = small[:part_h, :64], small[:part_h, 64:]
    channels = jnp.concatenate([low, high, jnp.zeros((128 - part0, 64), F32)], axis=0)
    turned[...] = jnp.concatenate([channels, channels], axis=1).T
    for letter in range(4):
        gew[:, letter, :] = turned[16 * letter : 16 * letter + kernel_width, :part0]
    geb[...] = turned[15:16, :part0]
    ggain[...] = turned[31:32, :part0]
    for copy in copies:
        copy.wait()


def shape(dims, kind):
    return jax.ShapeDtypeStruct(dims, kind)


def fused(bases, embed_weight, embed_bias, norm_gain, proj_weight, proj_bias, cotangent):
    kernel_width = embed_weight.shape[0]
    length = bases.shape[1]
    half = length // 2
    part0, d1 = proj_weight.shape
    part1 = proj_bias.shape[0]
    dp, seq = 8, 4
    d0, part_h = part0 * dp, part0 // 2
    big = half // 3
    vmem, hbm = pl.BlockSpec(memory_space=pltpu.VMEM), pl.BlockSpec(memory_space=pl.ANY)
    dma = pltpu.SemaphoreType.DMA
    scratch = [
        ((half, d1), BF16),
        ((1, length), jnp.int32),
        (embed_weight.shape, BF16),
        ((1, part0), BF16),
        ((1, part0), BF16),
        ((1, part1), BF16),
        ((2, 128), jnp.int32),
        ((16, length), jnp.int32),
        ((length, 128), F32),
        ((2, half, 64), BF16),
        ((2, 128, d0), F32),
        ((2, half, d0), F32),
        ((2, half, d0), F32),
        ((2, half, 128), F32),
        ((half, d0), BF16),
        ((2, half, d0), BF16),
        ((2, big, d0), F32),
        ((8, d0), F32),
        ((128, 128), F32),
        ((part_h + 16, 128), BF16),
        ((dp, part_h + 16, 128), BF16),
        ((dp, 2, part_h, d1), BF16),
        ((half, d1), BF16),
        ((dp, 2, part_h, d1), BF16),
        ((2, 4, part_h, d1), BF16),
        ((2, 4, part_h, d1), BF16),
        ((2, 4, part_h, d1), BF16),
        ((2, part_h, d1), BF16),
        ((4, part_h, d1), BF16),
        ((2, part_h, d1), BF16),
        ((dp, part_h + 16, 128), BF16),
        ((dp, part_h + 16, 128), BF16),
        ((seq, part_h + 16, 128), BF16),
    ]
    pooled, gw, small = pl.pallas_call(
        functools.partial(fused_kernel, kernel_width),
        out_shape=(
            shape((half, d1), BF16), shape((part0, d1), F32), shape((part_h + 16, 128), F32)
        ),
        in_specs=[hbm] * 7,
        out_specs=(hbm, vmem, vmem),
        scratch_shapes=[pltpu.VMEM(dims, kind) for dims, kind in scratch]
        + [dma((n,)) for n in (72, 2, dp)]
        + [dma((dp, 2)), dma((2,)), dma((2, 4)), dma((4,)), dma((2,)), dma((dp,)), dma((seq,)), dma((9,))],
        compiler_params=pltpu.CompilerParams(
            collective_id=0, has_side_effects=True, vmem_limit_bytes=60 * 2**20
        ),
        name="fused_step",
    )(
        bases, embed_weight, embed_bias[None], norm_gain[None], proj_weight, proj_bias[None],
        cotangent[0],
    )
    outs = pl.pallas_call(
        functools.partial(finish_kernel, kernel_width),
        out_shape=(
            shape((half, d1), BF16),
            shape(embed_weight.shape, F32),
            shape((1, part0), F32),
            shape((1, part0), F32),
            shape((part0, d1), F32),
            shape((1, part1), F32),
        ),
        in_specs=[pl.BlockSpec(memory_space=pl.ANY), pl.BlockSpec(memory_space=pl.ANY), vmem],
        out_specs=(hbm, vmem, vmem, vmem, hbm, vmem),
        scratch_shapes=[pltpu.VMEM((128, 128), F32), dma((2,))],
        compiler_params=pltpu.CompilerParams(vmem_limit_bytes=60 * 2**20),
        name="finish_step",
    )(pooled, gw, small)
    return (outs[0][None], outs[1], outs[2][0], outs[3][0], outs[4], outs[5][0])


def with_halo(x, sides, width):
    for axis, dim in sides:
        devices, length = (lax.axis_size(axis), x.shape[dim])
        up = [(i, (i + 1) % devices) for i in range(devices - 1)]
        down = [(j, i) for i, j in up]
        last = lax.slice_in_dim(x, length - width, length, axis=dim)
        leading = lax.slice_in_dim(x, 0, width, axis=dim)
        before = lax.ppermute(last, axis, up)
        after = lax.ppermute(leading, axis, down)
        x = jnp.concatenate([before, x, after], axis=dim)
    return x


def plain(bases, embed_weight, embed_bias, norm_gain, proj_weight, proj_bias, cotangent):
    kernel_width = embed_weight.shape[0]
    row_count = bases.shape[1]
    codes = bases + 1
    padded = with_halo(codes, (("seq", 1),), kernel_width // 2)[0]
    full_embed, full_bias, full_gain, full_proj, full_proj_bias = (
        lax.all_gather(embed_weight, "dp", axis=2, tiled=True),
        lax.all_gather(embed_bias, "dp", axis=0, tiled=True),
        lax.all_gather(norm_gain, "dp", axis=0, tiled=True),
        lax.all_gather(proj_weight, "dp", axis=0, tiled=True),
        lax.all_gather(proj_bias, "dp", axis=0, tiled=True),
    )
    letters = jnp.arange(1, 5, dtype=jnp.int32)
    features = jnp.concatenate(
        [
            (padded[k : k + row_count, None] == letters).astype(jnp.bfloat16)
            for k in range(kernel_width)
        ],
        axis=1,
    )
    flat_weight = full_embed.reshape(kernel_width * 4, -1)
    embedded = (
        jnp.dot(features, flat_weight, preferred_element_type=jnp.float32)
        + full_bias.astype(jnp.float32)
    ).astype(jnp.bfloat16)
    values = embedded.astype(jnp.float32)
    inverse = lax.rsqrt(jnp.mean(values * values, axis=1, keepdims=True) + 1e-06)
    scaled = values * inverse
    normed = scaled * full_gain.astype(jnp.float32)
    activated = jax.nn.gelu(normed, approximate=True).astype(jnp.bfloat16)
    product = jnp.dot(activated, full_proj, preferred_element_type=jnp.float32)
    mixed = product + full_proj_bias.astype(jnp.float32)
    pooled = jnp.mean(mixed.reshape(row_count // 2, 2, -1), axis=1).astype(jnp.bfloat16)
    scale_factor = 0.5 / (row_count * lax.axis_size("seq") * lax.axis_size("dp"))
    grad_mixed = (jnp.repeat(cotangent[0].astype(jnp.float32), 2, axis=0) * scale_factor).astype(
        jnp.bfloat16
    )
    grad_proj_weight = lax.dot_general(
        activated, grad_mixed, (((0,), (0,)), ((), ())), preferred_element_type=jnp.float32
    )
    grad_proj_bias = jnp.sum(grad_mixed.astype(jnp.float32), axis=0)
    grad_activated = lax.dot_general(
        grad_mixed, full_proj, (((1,), (1,)), ((), ())), preferred_element_type=jnp.float32
    )
    _, pullback = jax.vjp(lambda v: jax.nn.gelu(v, approximate=True), normed)
    grad_normed = pullback(grad_activated)[0]
    grad_norm_gain = jnp.sum(grad_normed * scaled, axis=0)
    weighted = grad_normed * full_gain.astype(jnp.float32)
    grad_embedded = (
        inverse * (weighted - scaled * jnp.mean(weighted * scaled, axis=1, keepdims=True))
    ).astype(jnp.bfloat16)
    grad_embed_weight = lax.dot_general(
        features, grad_embedded, (((0,), (0,)), ((), ())), preferred_element_type=jnp.float32
    ).reshape(kernel_width, 4, -1)
    grad_embed_bias = jnp.sum(grad_embedded.astype(jnp.float32), axis=0)
    whole = lax.psum(
        (grad_embed_weight, grad_embed_bias, grad_norm_gain, grad_proj_weight, grad_proj_bias),
        "seq",
    )
    results = (
        lax.psum_scatter(whole[0], "dp", scatter_dimension=2, tiled=True),
        lax.psum_scatter(whole[1], "dp", scatter_dimension=0, tiled=True),
        lax.psum_scatter(whole[2], "dp", scatter_dimension=0, tiled=True),
        lax.psum_scatter(whole[3], "dp", scatter_dimension=0, tiled=True),
        lax.psum_scatter(whole[4], "dp", scatter_dimension=0, tiled=True),
    )
    return (pooled[None], results[0], results[1], results[2], results[3], results[4])


def solution(mesh):
    placed = (
        P("dp", "seq"),
        P(None, None, "dp"),
        P("dp"),
        P("dp"),
        P("dp", None),
        P("dp"),
        P("dp", "seq", None),
    )
    step = fused if (mesh.shape["dp"], mesh.shape["seq"]) == (8, 4) else plain
    return jax.shard_map(
        step,
        mesh=mesh,
        in_specs=placed,
        out_specs=(
            P("dp", "seq", None),
            P(None, None, "dp"),
            P("dp"),
            P("dp"),
            P("dp", None),
            P("dp"),
        ),
        check_vma=False,
    )
```

```python
import functools

import jax
import jax.numpy as jnp
from jax import lax
from jax.experimental import pallas as pl
from jax.experimental.pallas import tpu as pltpu
from jax.sharding import PartitionSpec as P

F32, BF16 = jnp.float32, jnp.bfloat16
CUBIC = 0.044715
ROOT = 0.7978845608028654
NN = (((1,), (0,)), ((), ()))
NT = (((1,), (1,)), ((), ()))
TN = (((0,), (0,)), ((), ()))
MESH = pl.DeviceIdType.MESH
STEP = 16
PIECES = 4


def dot(a, b, dims):
    return lax.dot_general(a, b, dims, preferred_element_type=F32)


def build_features(bases_ref, halo_ref, stack_ref, wide_ref, feat_ref, kernel_width):
    length = bases_ref.shape[1]
    half, total = length // 2, length + 256
    ext = jnp.concatenate([halo_ref[0:1], bases_ref[...] + 1, halo_ref[1:2]], axis=1)
    ext = jnp.broadcast_to(ext, (8, total))
    for k in range(kernel_width):
        shift = k - kernel_width // 2
        moved = ext if shift == 0 else pltpu.roll(ext, (-shift) % total, 1)
        stack_ref[k : k + 1, :] = moved[0:1, 128 : 128 + length]
    stack_ref[kernel_width : kernel_width + 1, :] = jnp.ones((1, length), jnp.int32)
    stack = stack_ref[...]
    hot = jnp.concatenate([jnp.where(stack == c + 1, 1.0, 0.0) for c in range(4)] * 2, axis=0)
    wide_ref[...] = hot.T
    for parity in range(2):
        feat_ref[parity] = wide_ref[pl.ds(parity, half, stride=2), :][:, :64].astype(BF16)


def forward_chunk(start, size, feat_ref, weight, gain, emb_ref, scaled_ref, slope_ref, inv_ref, pact_ref):
    for parity in range(2):
        emb_ref[parity] = dot(feat_ref[parity, pl.ds(start, size), :], weight, NT)
    for r in range(0, size, STEP):
        rows = pl.ds(start + r, STEP)
        total = None
        for parity in range(2):
            emb = emb_ref[parity, r : r + STEP, :].astype(BF16).astype(F32)
            inverse = lax.rsqrt(jnp.mean(emb * emb, axis=1, keepdims=True) + 1e-6)
            scaled = emb * inverse
            x = scaled * gain
            sq = x * x
            t = 0.5 + 0.5 * jnp.tanh(x * (ROOT + (ROOT * CUBIC) * sq))
            act = x * t
            slope = t + act * (1.0 - t) * (2.0 * ROOT + (6.0 * ROOT * CUBIC) * sq)
            scaled_ref[parity, rows, :] = scaled
            slope_ref[parity, rows, :] = slope
            inv_ref[parity, rows, :] = jnp.broadcast_to(inverse, (STEP, 128))
            total = act if total is None else total + act
        pact_ref[rows, :] = total.astype(BF16)


def backward_chunk(start, size, cot_ref, w, gain, ga_ref, scaled_ref, slope_ref, inv_ref, ge_ref, acc_ref):
    ga_ref[...] = dot(cot_ref[start : start + size, :], w, NT)
    width = ga_ref.shape[1]
    acc = acc_ref[...]
    for r in range(0, size, STEP):
        rows = slice(start + r, start + r + STEP)
        ga = ga_ref[r : r + STEP, :]
        for parity in range(2):
            scaled = scaled_ref[parity, rows, :]
            inverse = inv_ref[parity, rows, 0:1]
            u = ga * slope_ref[parity, rows, :]
            q = u * scaled
            acc = acc + (q[:8] + q[8:])
            mean = jnp.sum(q * gain, axis=1, keepdims=True) * (1.0 / width)
            ge = inverse * (u * gain - scaled * mean)
            ge_ref[parity, rows, :] = ge.astype(BF16)
    acc_ref[...] = acc


def fused_kernel(
    kernel_width,
    bases_hbm, ew_hbm, eb_hbm, gain_hbm, w_hbm, pb_hbm, cot_hbm,
    pooled_hbm, gw_ref, small_out,
    pooled, bases, ew, eb, gain_in, pb, halo, stack, wide, feat, emb, scaled, slope, inv, pact, ge, ga, acc,
    rows_in, pack, packs, wbuf, cot, gwb, s1buf, p1, s2buf, sum2, s3buf, fin, small, sbuf, tbuf,
    send_sem, halo_recv, pack_recv, w_recv, s1_recv, s2_recv, s3_recv, fin_recv,
    small_recv, t_recv, local_sem,
):
    dp, seq = 8, 4
    length = bases.shape[1]
    half = length // 2
    part0, d1 = w_hbm.shape
    d0, part1, part_h = part0 * dp, d1 // dp, part0 // 2
    me, pos = lax.axis_index("dp"), lax.axis_index("seq")
    z, y, x, c = me // 2, me % 2, pos // 2, pos % 2
    y2, x2, c2 = 1 - y, 1 - x, 1 - c
    mate, across, skew = 2 * x + c2, 2 * x2 + c, 2 * x2 + c2
    own_rank = z % 2 == x
    factor = 0.25 / (half * seq * dp)

    barrier = pltpu.get_barrier_semaphore()
    for j in range(1, dp):
        pl.semaphore_signal(
            barrier, inc=1, device_id={"dp": (me + j) % dp, "seq": pos}, device_id_type=MESH
        )
    for j in range(1, seq):
        for to in (me, 2 * z + y2):
            pl.semaphore_signal(
                barrier, inc=1, device_id={"dp": to, "seq": (pos + j) % seq}, device_id_type=MESH
            )

    loads = [
        pltpu.make_async_copy(src, dst, local_sem.at[i])
        for i, (src, dst) in enumerate(
            [
                (ew_hbm, ew), (eb_hbm, eb), (gain_hbm, gain_in), (pb_hbm, pb), (bases_hbm, bases),
                (w_hbm.at[:part_h], wbuf.at[me, 0]), (w_hbm.at[part_h:], wbuf.at[me, 1]),
                (cot_hbm, cot),
            ]
        )
    ]
    for load in loads:
        load.start()
    rows_in[...] = jnp.zeros_like(rows_in)
    acc[...] = jnp.zeros_like(acc)
    for load in loads[:4]:
        load.wait()
    values = ew[...].astype(F32)
    for letter in range(4):
        rows_in[16 * letter : 16 * letter + kernel_width, :part0] = values[:, letter, :]
    rows_in[15:16, :part0] = eb[...].astype(F32)
    rows_in[31:32, :part0] = gain_in[...].astype(F32)
    turned = rows_in[...].T
    pack[:part_h, :] = jnp.concatenate(
        [turned[:part_h, :64], turned[part_h:part0, :64]], axis=1
    ).astype(BF16)
    tail = jnp.concatenate([pb[...].astype(F32), jnp.zeros((1, 128 - part1), F32)], axis=1)
    pack[part_h:, :] = jnp.broadcast_to(tail, (16, 128)).astype(BF16)
    packs[me] = pack[...]
    for load in loads[4:7]:
        load.wait()

    pl.semaphore_wait(barrier, dp - 1 + 2 * (seq - 1))

    started = []

    def send(src, dst, recv, to_dp, to_seq, pred=None):
        copy = pltpu.make_async_remote_copy(
            src_ref=src, dst_ref=dst, send_sem=send_sem.at[len(started)], recv_sem=recv,
            device_id={"dp": to_dp, "seq": to_seq}, device_id_type=MESH,
        )
        started.append((copy, pred))
        if pred is None:
            copy.start()
        else:
            pl.when(pred)(lambda: copy.start())

    def arrive(dst, recv, pred=None):
        copy = pltpu.make_async_remote_copy(
            src_ref=dst, dst_ref=dst, send_sem=send_sem.at[0], recv_sem=recv,
            device_id={"dp": me, "seq": mate}, device_id_type=MESH,
        )
        if pred is None:
            copy.wait_recv()
        else:
            pl.when(pred)(lambda: copy.wait_recv())

    send(bases.at[:, length - 128 :], halo.at[0:1], halo_recv.at[0], me, pos + 1, pos < seq - 1)
    send(bases.at[:, :128], halo.at[1:2], halo_recv.at[1], me, pos - 1, pos > 0)
    for j in range(1, dp):
        send(pack, packs.at[me], pack_recv.at[me], (me + j) % dp, pos)
    for zz in range(4):
        send(wbuf.at[me, c], wbuf.at[me, c], w_recv.at[me, c], 2 * zz + y, pos, z != zz)
    send(wbuf.at[me, c], wbuf.at[me, c], w_recv.at[me, c], 2 * z + y2, pos)

    arrive(halo.at[0:1], halo_recv.at[0], pos > 0)
    arrive(halo.at[1:2], halo_recv.at[1], pos < seq - 1)
    for side, edge in ((0, 0), (1, seq - 1)):

        @pl.when(pos == edge)
        def _(side=side):
            halo[side : side + 1, :] = jnp.zeros((1, 128), jnp.int32)

        @pl.when(pos != edge)
        def _(side=side):
            halo[side : side + 1, :] = halo[side : side + 1, :] + 1


    build_features(bases, halo, stack, wide, feat, kernel_width)
    for j in range(1, dp):
        arrive(packs.at[(me + j) % dp], pack_recv.at[(me + j) % dp])
    weight = jnp.concatenate(
        [packs[d, :part_h, 64 * h : 64 * h + 64] for d in range(dp) for h in range(2)], axis=0
    )
    lanes = lax.broadcasted_iota(jnp.int32, (16, 64), 1)
    gain = dot(jnp.where(lanes == 31, 1.0, 0.0).astype(BF16), weight, NT)[0:1]
    size = 128
    chunks = half // size

    def forward(first, last):
        @pl.loop(first, last)
        def _(i):
            start = pl.multiple_of(i * size, size)
            forward_chunk(start, size, feat, weight, gain, emb, scaled, slope, inv, pact)

    def relay(distances):
        for zz in range(4):
            d = 2 * zz + y
            slot, sem = wbuf.at[d, c], w_recv.at[d, c]
            for distance in distances:
                there = (z == zz - distance) | (z == zz + distance)
                arrive(slot, sem, there)
                send(slot, slot, sem, 2 * z + y2, pos, there)
                send(slot, slot, sem, me, mate, there)

    forward(0, chunks // 3)
    relay((1,))
    d = 2 * z + y2
    arrive(wbuf.at[d, c], w_recv.at[d, c])
    send(wbuf.at[d, c], wbuf.at[d, c], w_recv.at[d, c], me, mate)
    forward(chunks // 3, 2 * chunks // 3)
    relay((2, 3))
    forward(2 * chunks // 3, chunks)

    loads[7].wait()
    block = d0 // 2
    for b in range(2):
        value = dot(pact[:, b * block : (b + 1) * block], cot[...], TN)
        gwb[4 * b : 4 * b + 4] = value.astype(BF16).reshape(4, 2, part_h, d1)
        send(gwb.at[4 * b : 4 * b + 4, c2], s1buf.at[b], s1_recv.at[b], me, mate)

    for zz in range(4):
        d = 2 * zz + y2
        slot, sem = wbuf.at[d, c], w_recv.at[d, c]
        arrive(slot, sem, z != zz)
        send(slot, slot, sem, me, mate, z != zz)

    rank = 2 * x + y
    others = (
        (2 * x2 + y2, 2 * z + y2, across),
        (2 * x + y2, 2 * z + y2, pos),
        (2 * x2 + y, me, across),
    )
    for b in range(2):
        arrive(s1buf.at[b], s1_recv.at[b])
        for k in range(4):
            p1[b, k] = (gwb[4 * b + k, c].astype(F32) + s1buf[b, k].astype(F32)).astype(BF16)
        for piece, to_dp, to_seq in others:
            send(p1.at[b, piece], s2buf.at[b, rank], s2_recv.at[b, rank], to_dp, to_seq)

    for d in range(dp):
        arrive(wbuf.at[d, c2], w_recv.at[d, c2], me != d)

    tails = [packs[d, part_h:, :].astype(F32)[:8, :part1] for d in range(dp)]
    bias = jnp.concatenate(tails, axis=1)[0:1]

    big = half // 3
    for i in range(3):
        w = wbuf[...].reshape(d0, d1)
        value = 0.5 * dot(pact[i * big : (i + 1) * big, :], w, NN) + bias
        pooled[i * big : (i + 1) * big, :] = value.astype(BF16)
    pooled_out = pltpu.make_async_copy(pooled, pooled_hbm, local_sem.at[8])
    pooled_out.start()

    def backward(i):
        w = wbuf[...].reshape(d0, d1)
        backward_chunk(i * big, big, cot, w, gain, ga.at[i % 2], scaled, slope, inv, ge, acc)

    def plane_sum(k):
        total = p1[k, rank].astype(F32)
        for piece, _, _ in others:
            arrive(s2buf.at[k, piece], s2_recv.at[k, piece])
            total = total + s2buf[k, piece].astype(F32)
        sum2[k] = total.astype(BF16)
        zt = x + 2 * k
        send(sum2.at[k], s3buf.at[z], s3_recv.at[z], 2 * zt + y, pos, zt != z)

    backward(0)
    backward(1)
    plane_sum(0)
    backward(2)
    plane_sum(1)

    g = dot(feat[0], ge[0], TN) + dot(feat[1], ge[1], TN)
    gain_row = jnp.sum(acc[...], axis=0, keepdims=True)
    g = jnp.where(lax.broadcasted_iota(jnp.int32, (64, d0), 0) == 31, gain_row, g)
    turned = jnp.concatenate([g, jnp.zeros_like(g)], axis=0).T
    for d in range(dp):
        low = turned[d * part0 : d * part0 + part_h, :64]
        high = turned[d * part0 + part_h : (d + 1) * part0, :64]
        small[d, :part_h, :] = jnp.concatenate([low, high], axis=1).astype(BF16)
    sums = 2.0 * dot(jnp.ones((16, half), BF16), cot[...], NN)[0:8]
    for d in range(dp):
        own = jnp.concatenate(
            [sums[:, d * part1 : (d + 1) * part1], jnp.zeros((8, 128 - part1), F32)], axis=1
        )
        small[d, part_h:, :] = jnp.concatenate([own, own], axis=0).astype(BF16)
    for j in range(1, dp):
        to = (me + j) % dp
        send(small.at[to], sbuf.at[me], small_recv.at[me], to, pos)
    sbuf[me] = small[me]

    for zz in range(4):
        arrive(s3buf.at[zz], s3_recv.at[zz], own_rank & (z != zz))

    @pl.when(own_rank)
    def _():
        value = sum2[z // 2].astype(F32)
        for j in range(1, 4):
            value = value + s3buf[(z + j) % 4].astype(F32)
        fin[c] = value.astype(BF16)

    send(fin.at[c], fin.at[c], fin_recv.at[c], me, across, own_rank)
    arrive(fin.at[c], fin_recv.at[c], jnp.logical_not(own_rank))
    send(fin.at[c], fin.at[c], fin_recv.at[c], me, mate)

    for j in range(1, dp):
        arrive(sbuf.at[(me + j) % dp], small_recv.at[(me + j) % dp])
    tbuf[pos] = jnp.sum(sbuf[...].astype(F32), axis=0).astype(BF16)
    for j in range(1, seq):
        send(tbuf.at[pos], tbuf.at[pos], t_recv.at[pos], me, (pos + j) % seq)

    arrive(fin.at[c2], fin_recv.at[c2])
    gw_ref[...] = fin[...].astype(F32).reshape(part0, d1) * factor
    for j in range(1, seq):
        arrive(tbuf.at[(pos + j) % seq], t_recv.at[(pos + j) % seq])
    small_out[...] = jnp.sum(tbuf[...].astype(F32), axis=0) * factor

    for copy, pred in started:
        if pred is None:
            copy.wait_send()
        else:
            pl.when(pred)(lambda copy=copy: copy.wait_send())
    pooled_out.wait()


def finish_kernel(kernel_width, pooled_in, gw_in, small, pooled, gew, geb, ggain, gw, gpb, turned, held, held_gw, sems):
    part0, part1 = gw_in.shape[0], gpb.shape[1]
    part_h = part0 // 2
    rows = pooled_in.shape[0] // PIECES
    pieces = [
        (pooled_in.at[pl.ds(i * rows, rows)], held.at[pl.ds(i * rows, rows)], pooled.at[pl.ds(i * rows, rows)])
        for i in range(PIECES)
    ] + [(gw_in, held_gw, gw)]
    loads = [pltpu.make_async_copy(src, mid, sems.at[0, i]) for i, (src, mid, _) in enumerate(pieces)]
    stores = [pltpu.make_async_copy(mid, dst, sems.at[1, i]) for i, (_, mid, dst) in enumerate(pieces)]
    for load in loads:
        load.start()
    for load, store in zip(loads, stores):
        load.wait()
        store.start()
    gpb[...] = small[part_h : part_h + 1, :part1]
    low, high = small[:part_h, :64], small[:part_h, 64:]
    channels = jnp.concatenate([low, high, jnp.zeros((128 - part0, 64), F32)], axis=0)
    turned[...] = jnp.concatenate([channels, channels], axis=1).T
    for letter in range(4):
        gew[:, letter, :] = turned[16 * letter : 16 * letter + kernel_width, :part0]
    geb[...] = turned[15:16, :part0]
    ggain[...] = turned[31:32, :part0]
    for store in stores:
        store.wait()


def shape(dims, kind):
    return jax.ShapeDtypeStruct(dims, kind)


def fused(bases, embed_weight, embed_bias, norm_gain, proj_weight, proj_bias, cotangent):
    kernel_width = embed_weight.shape[0]
    length = bases.shape[1]
    half = length // 2
    part0, d1 = proj_weight.shape
    part1 = proj_bias.shape[0]
    dp, seq = 8, 4
    d0, part_h = part0 * dp, part0 // 2
    big = half // 3
    vmem, hbm = pl.BlockSpec(memory_space=pltpu.VMEM), pl.BlockSpec(memory_space=pl.ANY)
    dma = pltpu.SemaphoreType.DMA
    scratch = [
        ((half, d1), BF16),
        ((1, length), jnp.int32),
        (embed_weight.shape, BF16),
        ((1, part0), BF16),
        ((1, part0), BF16),
        ((1, part1), BF16),
        ((2, 128), jnp.int32),
        ((16, length), jnp.int32),
        ((length, 128), F32),
        ((2, half, 64), BF16),
        ((2, 128, d0), F32),
        ((2, half, d0), F32),
        ((2, half, d0), F32),
        ((2, half, 128), F32),
        ((half, d0), BF16),
        ((2, half, d0), BF16),
        ((2, big, d0), F32),
        ((8, d0), F32),
        ((128, 128), F32),
        ((part_h + 16, 128), BF16),
        ((dp, part_h + 16, 128), BF16),
        ((dp, 2, part_h, d1), BF16),
        ((half, d1), BF16),
        ((dp, 2, part_h, d1), BF16),
        ((2, 4, part_h, d1), BF16),
        ((2, 4, part_h, d1), BF16),
        ((2, 4, part_h, d1), BF16),
        ((2, part_h, d1), BF16),
        ((4, part_h, d1), BF16),
        ((2, part_h, d1), BF16),
        ((dp, part_h + 16, 128), BF16),
        ((dp, part_h + 16, 128), BF16),
        ((seq, part_h + 16, 128), BF16),
    ]
    pooled, gw, small = pl.pallas_call(
        functools.partial(fused_kernel, kernel_width),
        out_shape=(
            shape((half, d1), BF16), shape((part0, d1), F32), shape((part_h + 16, 128), F32)
        ),
        in_specs=[hbm] * 7,
        out_specs=(hbm, vmem, vmem),
        scratch_shapes=[pltpu.VMEM(dims, kind) for dims, kind in scratch]
        + [dma((n,)) for n in (72, 2, dp)]
        + [dma((dp, 2)), dma((2,)), dma((2, 4)), dma((4,)), dma((2,)), dma((dp,)), dma((seq,)), dma((9,))],
        compiler_params=pltpu.CompilerParams(
            collective_id=0, has_side_effects=True, vmem_limit_bytes=60 * 2**20
        ),
        name="fused_step",
    )(
        bases, embed_weight, embed_bias[None], norm_gain[None], proj_weight, proj_bias[None],
        cotangent[0],
    )
    outs = pl.pallas_call(
        functools.partial(finish_kernel, kernel_width),
        out_shape=(
            shape((half, d1), BF16),
            shape(embed_weight.shape, F32),
            shape((1, part0), F32),
            shape((1, part0), F32),
            shape((part0, d1), F32),
            shape((1, part1), F32),
        ),
        in_specs=[pl.BlockSpec(memory_space=pl.ANY), pl.BlockSpec(memory_space=pl.ANY), vmem],
        out_specs=(hbm, vmem, vmem, vmem, hbm, vmem),
        scratch_shapes=[
            pltpu.VMEM((128, 128), F32),
            pltpu.VMEM((half, d1), BF16),
            pltpu.VMEM((part0, d1), F32),
            dma((2, PIECES + 1)),
        ],
        compiler_params=pltpu.CompilerParams(vmem_limit_bytes=60 * 2**20),
        name="finish_step",
    )(pooled, gw, small)
    return (outs[0][None], outs[1], outs[2][0], outs[3][0], outs[4], outs[5][0])


def with_halo(x, sides, width):
    for axis, dim in sides:
        devices, length = (lax.axis_size(axis), x.shape[dim])
        up = [(i, (i + 1) % devices) for i in range(devices - 1)]
        down = [(j, i) for i, j in up]
        last = lax.slice_in_dim(x, length - width, length, axis=dim)
        leading = lax.slice_in_dim(x, 0, width, axis=dim)
        before = lax.ppermute(last, axis, up)
        after = lax.ppermute(leading, axis, down)
        x = jnp.concatenate([before, x, after], axis=dim)
    return x


def plain(bases, embed_weight, embed_bias, norm_gain, proj_weight, proj_bias, cotangent):
    kernel_width = embed_weight.shape[0]
    row_count = bases.shape[1]
    codes = bases + 1
    padded = with_halo(codes, (("seq", 1),), kernel_width // 2)[0]
    full_embed, full_bias, full_gain, full_proj, full_proj_bias = (
        lax.all_gather(embed_weight, "dp", axis=2, tiled=True),
        lax.all_gather(embed_bias, "dp", axis=0, tiled=True),
        lax.all_gather(norm_gain, "dp", axis=0, tiled=True),
        lax.all_gather(proj_weight, "dp", axis=0, tiled=True),
        lax.all_gather(proj_bias, "dp", axis=0, tiled=True),
    )
    letters = jnp.arange(1, 5, dtype=jnp.int32)
    features = jnp.concatenate(
        [
            (padded[k : k + row_count, None] == letters).astype(jnp.bfloat16)
            for k in range(kernel_width)
        ],
        axis=1,
    )
    flat_weight = full_embed.reshape(kernel_width * 4, -1)
    embedded = (
        jnp.dot(features, flat_weight, preferred_element_type=jnp.float32)
        + full_bias.astype(jnp.float32)
    ).astype(jnp.bfloat16)
    values = embedded.astype(jnp.float32)
    inverse = lax.rsqrt(jnp.mean(values * values, axis=1, keepdims=True) + 1e-06)
    scaled = values * inverse
    normed = scaled * full_gain.astype(jnp.float32)
    activated = jax.nn.gelu(normed, approximate=True).astype(jnp.bfloat16)
    product = jnp.dot(activated, full_proj, preferred_element_type=jnp.float32)
    mixed = product + full_proj_bias.astype(jnp.float32)
    pooled = jnp.mean(mixed.reshape(row_count // 2, 2, -1), axis=1).astype(jnp.bfloat16)
    scale_factor = 0.5 / (row_count * lax.axis_size("seq") * lax.axis_size("dp"))
    grad_mixed = (jnp.repeat(cotangent[0].astype(jnp.float32), 2, axis=0) * scale_factor).astype(
        jnp.bfloat16
    )
    grad_proj_weight = lax.dot_general(
        activated, grad_mixed, (((0,), (0,)), ((), ())), preferred_element_type=jnp.float32
    )
    grad_proj_bias = jnp.sum(grad_mixed.astype(jnp.float32), axis=0)
    grad_activated = lax.dot_general(
        grad_mixed, full_proj, (((1,), (1,)), ((), ())), preferred_element_type=jnp.float32
    )
    _, pullback = jax.vjp(lambda v: jax.nn.gelu(v, approximate=True), normed)
    grad_normed = pullback(grad_activated)[0]
    grad_norm_gain = jnp.sum(grad_normed * scaled, axis=0)
    weighted = grad_normed * full_gain.astype(jnp.float32)
    grad_embedded = (
        inverse * (weighted - scaled * jnp.mean(weighted * scaled, axis=1, keepdims=True))
    ).astype(jnp.bfloat16)
    grad_embed_weight = lax.dot_general(
        features, grad_embedded, (((0,), (0,)), ((), ())), preferred_element_type=jnp.float32
    ).reshape(kernel_width, 4, -1)
    grad_embed_bias = jnp.sum(grad_embedded.astype(jnp.float32), axis=0)
    whole = lax.psum(
        (grad_embed_weight, grad_embed_bias, grad_norm_gain, grad_proj_weight, grad_proj_bias),
        "seq",
    )
    results = (
        lax.psum_scatter(whole[0], "dp", scatter_dimension=2, tiled=True),
        lax.psum_scatter(whole[1], "dp", scatter_dimension=0, tiled=True),
        lax.psum_scatter(whole[2], "dp", scatter_dimension=0, tiled=True),
        lax.psum_scatter(whole[3], "dp", scatter_dimension=0, tiled=True),
        lax.psum_scatter(whole[4], "dp", scatter_dimension=0, tiled=True),
    )
    return (pooled[None], results[0], results[1], results[2], results[3], results[4])


def solution(mesh):
    placed = (
        P("dp", "seq"),
        P(None, None, "dp"),
        P("dp"),
        P("dp"),
        P("dp", None),
        P("dp"),
        P("dp", "seq", None),
    )
    step = fused if (mesh.shape["dp"], mesh.shape["seq"]) == (8, 4) else plain
    return jax.shard_map(
        step,
        mesh=mesh,
        in_specs=placed,
        out_specs=(
            P("dp", "seq", None),
            P(None, None, "dp"),
            P("dp"),
            P("dp"),
            P("dp", None),
            P("dp"),
        ),
        check_vma=False,
    )
```

```python
import functools

import jax
import jax.numpy as jnp
from jax import lax
from jax.experimental import pallas as pl
from jax.experimental.pallas import tpu as pltpu
from jax.sharding import PartitionSpec as P

F32, BF16 = jnp.float32, jnp.bfloat16
CUBIC = 0.044715
ROOT = 0.7978845608028654
NN = (((1,), (0,)), ((), ()))
NT = (((1,), (1,)), ((), ()))
TN = (((0,), (0,)), ((), ()))
MESH = pl.DeviceIdType.MESH
STEP = 16
PIECES = 4


def dot(a, b, dims):
    return lax.dot_general(a, b, dims, preferred_element_type=F32)


def build_features(bases_ref, halo_ref, stack_ref, wide_ref, feat_ref, kernel_width):
    length = bases_ref.shape[1]
    half, total = length // 2, length + 256
    ext = jnp.concatenate([halo_ref[0:1], bases_ref[...] + 1, halo_ref[1:2]], axis=1)
    ext = jnp.broadcast_to(ext, (8, total))
    for k in range(kernel_width):
        shift = k - kernel_width // 2
        moved = ext if shift == 0 else pltpu.roll(ext, (-shift) % total, 1)
        stack_ref[k : k + 1, :] = moved[0:1, 128 : 128 + length]
    stack_ref[kernel_width : kernel_width + 1, :] = jnp.ones((1, length), jnp.int32)
    stack = stack_ref[...]
    hot = jnp.concatenate([jnp.where(stack == c + 1, 1.0, 0.0) for c in range(4)] * 2, axis=0)
    wide_ref[...] = hot.T
    for parity in range(2):
        feat_ref[parity] = wide_ref[pl.ds(parity, half, stride=2), :][:, :64].astype(BF16)


def forward_chunk(start, size, feat_ref, weight, gain, emb_ref, scaled_ref, slope_ref, inv_ref, pact_ref):
    for parity in range(2):
        emb_ref[parity] = dot(feat_ref[parity, pl.ds(start, size), :], weight, NT)
    for r in range(0, size, STEP):
        rows = pl.ds(start + r, STEP)
        total = None
        for parity in range(2):
            emb = emb_ref[parity, r : r + STEP, :].astype(BF16).astype(F32)
            inverse = lax.rsqrt(jnp.mean(emb * emb, axis=1, keepdims=True) + 1e-6)
            scaled = emb * inverse
            x = scaled * gain
            sq = x * x
            t = 0.5 + 0.5 * jnp.tanh(x * (ROOT + (ROOT * CUBIC) * sq))
            act = x * t
            slope = t + act * (1.0 - t) * (2.0 * ROOT + (6.0 * ROOT * CUBIC) * sq)
            scaled_ref[parity, rows, :] = scaled
            slope_ref[parity, rows, :] = slope
            inv_ref[parity, rows, :] = jnp.broadcast_to(inverse, (STEP, 128))
            total = act if total is None else total + act
        pact_ref[rows, :] = total.astype(BF16)


def backward_chunk(start, size, cot_ref, w, gain, ga_ref, scaled_ref, slope_ref, inv_ref, ge_ref, acc_ref):
    ga_ref[...] = dot(cot_ref[start : start + size, :], w, NT)
    width = ga_ref.shape[1]
    acc = acc_ref[...]
    for r in range(0, size, STEP):
        rows = slice(start + r, start + r + STEP)
        ga = ga_ref[r : r + STEP, :]
        for parity in range(2):
            scaled = scaled_ref[parity, rows, :]
            inverse = inv_ref[parity, rows, 0:1]
            u = ga * slope_ref[parity, rows, :]
            q = u * scaled
            acc = acc + (q[:8] + q[8:])
            mean = jnp.sum(q * gain, axis=1, keepdims=True) * (1.0 / width)
            ge = inverse * (u * gain - scaled * mean)
            ge_ref[parity, rows, :] = ge.astype(BF16)
    acc_ref[...] = acc


def fused_kernel(
    kernel_width,
    bases_hbm, ew_hbm, eb_hbm, gain_hbm, w_hbm, pb_hbm, cot_hbm,
    pooled_hbm, gw_ref, small_out,
    pooled, bases, ew, eb, gain_in, pb, halo, stack, wide, feat, emb, scaled, slope, inv, pact, ge, ga, acc,
    rows_in, pack, packs, wbuf, cot, gwb, s1buf, p1, s2buf, sum2, s3buf, fin, small, sbuf, tbuf,
    send_sem, halo_recv, pack_recv, w_recv, s1_recv, s2_recv, s3_recv, fin_recv,
    small_recv, t_recv, local_sem,
):
    dp, seq = 8, 4
    length = bases.shape[1]
    half = length // 2
    part0, d1 = w_hbm.shape
    d0, part1, part_h = part0 * dp, d1 // dp, part0 // 2
    me, pos = lax.axis_index("dp"), lax.axis_index("seq")
    z, y, x, c = me // 2, me % 2, pos // 2, pos % 2
    y2, x2, c2 = 1 - y, 1 - x, 1 - c
    mate, across, skew = 2 * x + c2, 2 * x2 + c, 2 * x2 + c2
    own_rank = z % 2 == x
    factor = 0.25 / (half * seq * dp)

    barrier = pltpu.get_barrier_semaphore()
    for j in range(1, dp):
        pl.semaphore_signal(
            barrier, inc=1, device_id={"dp": (me + j) % dp, "seq": pos}, device_id_type=MESH
        )
    for j in range(1, seq):
        for to in (me, 2 * z + y2):
            pl.semaphore_signal(
                barrier, inc=1, device_id={"dp": to, "seq": (pos + j) % seq}, device_id_type=MESH
            )

    loads = [
        pltpu.make_async_copy(src, dst, local_sem.at[i])
        for i, (src, dst) in enumerate(
            [
                (ew_hbm, ew), (eb_hbm, eb), (gain_hbm, gain_in), (pb_hbm, pb), (bases_hbm, bases),
                (w_hbm.at[:part_h], wbuf.at[me, 0]), (w_hbm.at[part_h:], wbuf.at[me, 1]),
                (cot_hbm, cot),
            ]
        )
    ]
    for load in loads:
        load.start()
    rows_in[...] = jnp.zeros_like(rows_in)
    acc[...] = jnp.zeros_like(acc)
    for load in loads[:4]:
        load.wait()
    values = ew[...].astype(F32)
    for letter in range(4):
        rows_in[16 * letter : 16 * letter + kernel_width, :part0] = values[:, letter, :]
    rows_in[15:16, :part0] = eb[...].astype(F32)
    rows_in[31:32, :part0] = gain_in[...].astype(F32)
    turned = rows_in[...].T
    pack[:part_h, :] = jnp.concatenate(
        [turned[:part_h, :64], turned[part_h:part0, :64]], axis=1
    ).astype(BF16)
    tail = jnp.concatenate([pb[...].astype(F32), jnp.zeros((1, 128 - part1), F32)], axis=1)
    pack[part_h:, :] = jnp.broadcast_to(tail, (16, 128)).astype(BF16)
    packs[me] = pack[...]
    for load in loads[4:7]:
        load.wait()

    pl.semaphore_wait(barrier, dp - 1 + 2 * (seq - 1))

    started = []

    def send(src, dst, recv, to_dp, to_seq, pred=None):
        copy = pltpu.make_async_remote_copy(
            src_ref=src, dst_ref=dst, send_sem=send_sem.at[len(started)], recv_sem=recv,
            device_id={"dp": to_dp, "seq": to_seq}, device_id_type=MESH,
        )
        started.append((copy, pred))
        if pred is None:
            copy.start()
        else:
            pl.when(pred)(lambda: copy.start())

    def arrive(dst, recv, pred=None):
        copy = pltpu.make_async_remote_copy(
            src_ref=dst, dst_ref=dst, send_sem=send_sem.at[0], recv_sem=recv,
            device_id={"dp": me, "seq": mate}, device_id_type=MESH,
        )
        if pred is None:
            copy.wait_recv()
        else:
            pl.when(pred)(lambda: copy.wait_recv())

    send(bases.at[:, length - 128 :], halo.at[0:1], halo_recv.at[0], me, pos + 1, pos < seq - 1)
    send(bases.at[:, :128], halo.at[1:2], halo_recv.at[1], me, pos - 1, pos > 0)
    for j in range(1, dp):
        send(pack, packs.at[me], pack_recv.at[me], (me + j) % dp, pos)
    send(wbuf.at[me, c], wbuf.at[me, c], w_recv.at[me, c], 2 * z + y2, pos)

    def shard_out(distances):
        for zz in range(4):
            for distance in distances:
                there = (z == zz - distance) | (z == zz + distance)
                send(wbuf.at[me, c], wbuf.at[me, c], w_recv.at[me, c], 2 * zz + y, pos, there)

    shard_out((1,))

    arrive(halo.at[0:1], halo_recv.at[0], pos > 0)
    arrive(halo.at[1:2], halo_recv.at[1], pos < seq - 1)
    for side, edge in ((0, 0), (1, seq - 1)):

        @pl.when(pos == edge)
        def _(side=side):
            halo[side : side + 1, :] = jnp.zeros((1, 128), jnp.int32)

        @pl.when(pos != edge)
        def _(side=side):
            halo[side : side + 1, :] = halo[side : side + 1, :] + 1


    build_features(bases, halo, stack, wide, feat, kernel_width)
    for j in range(1, dp):
        arrive(packs.at[(me + j) % dp], pack_recv.at[(me + j) % dp])
    shard_out((3, 2))
    weight = jnp.concatenate(
        [packs[d, :part_h, 64 * h : 64 * h + 64] for d in range(dp) for h in range(2)], axis=0
    )
    lanes = lax.broadcasted_iota(jnp.int32, (16, 64), 1)
    gain = dot(jnp.where(lanes == 31, 1.0, 0.0).astype(BF16), weight, NT)[0:1]
    size = 256
    chunks = half // size

    def forward(first, last):
        @pl.loop(first, last)
        def _(i):
            start = pl.multiple_of(i * size, size)
            forward_chunk(start, size, feat, weight, gain, emb, scaled, slope, inv, pact)

    def relay(distances):
        for zz in range(4):
            d = 2 * zz + y
            slot, sem = wbuf.at[d, c], w_recv.at[d, c]
            for distance in distances:
                there = (z == zz - distance) | (z == zz + distance)
                arrive(slot, sem, there)
                send(slot, slot, sem, 2 * z + y2, pos, there)
                send(slot, slot, sem, me, mate, there)

    forward(0, chunks // 3)
    relay((1,))
    d = 2 * z + y2
    arrive(wbuf.at[d, c], w_recv.at[d, c])
    send(wbuf.at[d, c], wbuf.at[d, c], w_recv.at[d, c], me, mate)
    forward(chunks // 3, chunks)

    loads[7].wait()
    block = d0 // 2
    for b in range(2):
        value = dot(pact[:, b * block : (b + 1) * block], cot[...], TN)
        gwb[4 * b : 4 * b + 4] = value.astype(BF16).reshape(4, 2, part_h, d1)
        send(gwb.at[4 * b : 4 * b + 4, c2], s1buf.at[b], s1_recv.at[b], me, mate)
        if b == 0:
            relay((2, 3))

    rank = 2 * x + y
    others = (
        (2 * x2 + y2, 2 * z + y2, across),
        (2 * x + y2, 2 * z + y2, pos),
        (2 * x2 + y, me, across),
    )
    for b in range(2):
        arrive(s1buf.at[b], s1_recv.at[b])
        for k in range(4):
            p1[b, k] = (gwb[4 * b + k, c].astype(F32) + s1buf[b, k].astype(F32)).astype(BF16)
        for piece, to_dp, to_seq in others:
            send(p1.at[b, piece], s2buf.at[b, rank], s2_recv.at[b, rank], to_dp, to_seq)

    for zz in range(4):
        d = 2 * zz + y2
        slot, sem = wbuf.at[d, c], w_recv.at[d, c]
        arrive(slot, sem, z != zz)
        send(slot, slot, sem, me, mate, z != zz)

    for d in range(dp):
        arrive(wbuf.at[d, c2], w_recv.at[d, c2], me != d)

    tails = [packs[d, part_h:, :].astype(F32)[:8, :part1] for d in range(dp)]
    bias = jnp.concatenate(tails, axis=1)[0:1]

    big = half // 3
    for i in range(3):
        w = wbuf[...].reshape(d0, d1)
        value = 0.5 * dot(pact[i * big : (i + 1) * big, :], w, NN) + bias
        pooled[i * big : (i + 1) * big, :] = value.astype(BF16)
    pooled_out = pltpu.make_async_copy(pooled, pooled_hbm, local_sem.at[8])
    pooled_out.start()

    def backward(i):
        w = wbuf[...].reshape(d0, d1)
        backward_chunk(i * big, big, cot, w, gain, ga.at[i % 2], scaled, slope, inv, ge, acc)

    def plane_sum(k):
        total = p1[k, rank].astype(F32)
        for piece, _, _ in others:
            arrive(s2buf.at[k, piece], s2_recv.at[k, piece])
            total = total + s2buf[k, piece].astype(F32)
        sum2[k] = total.astype(BF16)
        zt = x + 2 * k
        send(sum2.at[k], s3buf.at[z], s3_recv.at[z], 2 * zt + y, pos, zt != z)

    backward(0)
    backward(1)
    plane_sum(0)
    backward(2)

    g = dot(feat[0], ge[0], TN) + dot(feat[1], ge[1], TN)
    gain_row = jnp.sum(acc[...], axis=0, keepdims=True)
    g = jnp.where(lax.broadcasted_iota(jnp.int32, (64, d0), 0) == 31, gain_row, g)
    turned = jnp.concatenate([g, jnp.zeros_like(g)], axis=0).T
    for d in range(dp):
        low = turned[d * part0 : d * part0 + part_h, :64]
        high = turned[d * part0 + part_h : (d + 1) * part0, :64]
        small[d, :part_h, :] = jnp.concatenate([low, high], axis=1).astype(BF16)
    sums = 2.0 * dot(jnp.ones((16, half), BF16), cot[...], NN)[0:8]
    for d in range(dp):
        own = jnp.concatenate(
            [sums[:, d * part1 : (d + 1) * part1], jnp.zeros((8, 128 - part1), F32)], axis=1
        )
        small[d, part_h:, :] = jnp.concatenate([own, own], axis=0).astype(BF16)
    for j in range(1, dp):
        to = (me + j) % dp
        send(small.at[to], sbuf.at[me], small_recv.at[me], to, pos)
    sbuf[me] = small[me]
    plane_sum(1)

    for zz in range(4):
        arrive(s3buf.at[zz], s3_recv.at[zz], own_rank & (z != zz))

    @pl.when(own_rank)
    def _():
        value = sum2[z // 2].astype(F32)
        for j in range(1, 4):
            value = value + s3buf[(z + j) % 4].astype(F32)
        fin[c] = value.astype(BF16)

    send(fin.at[c], fin.at[c], fin_recv.at[c], me, across, own_rank)
    arrive(fin.at[c], fin_recv.at[c], jnp.logical_not(own_rank))
    send(fin.at[c], fin.at[c], fin_recv.at[c], me, mate)

    for j in range(1, dp):
        arrive(sbuf.at[(me + j) % dp], small_recv.at[(me + j) % dp])
    tbuf[pos] = jnp.sum(sbuf[...].astype(F32), axis=0).astype(BF16)
    for j in range(1, seq):
        send(tbuf.at[pos], tbuf.at[pos], t_recv.at[pos], me, (pos + j) % seq)

    arrive(fin.at[c2], fin_recv.at[c2])
    gw_ref[...] = fin[...].astype(F32).reshape(part0, d1) * factor
    for j in range(1, seq):
        arrive(tbuf.at[(pos + j) % seq], t_recv.at[(pos + j) % seq])
    small_out[...] = jnp.sum(tbuf[...].astype(F32), axis=0) * factor

    for copy, pred in started:
        if pred is None:
            copy.wait_send()
        else:
            pl.when(pred)(lambda copy=copy: copy.wait_send())
    pooled_out.wait()


def finish_kernel(
    kernel_width, pooled_in, gw_in, small_in, pooled, gew, geb, ggain, gw, gpb,
    turned, held, held_gw, small, out_ew, out_eb, out_gain, out_pb, load_sem, store_sem,
):
    part0, part1 = gw_in.shape[0], gpb.shape[1]
    part_h = part0 // 2
    rows = pooled_in.shape[0] // PIECES
    pieces = [(small_in, small, None), (gw_in, held_gw, gw)]
    for i in range(PIECES):
        span = pl.ds(i * rows, rows)
        pieces.append((pooled_in.at[span], held.at[span], pooled.at[span]))
    loads = [
        pltpu.make_async_copy(src, mid, load_sem.at[i]) for i, (src, mid, _) in enumerate(pieces)
    ]
    for load in loads:
        load.start()
    stores = []

    def store(src, dst):
        copy = pltpu.make_async_copy(src, dst, store_sem.at[len(stores)])
        stores.append(copy)
        copy.start()

    for load, (_, mid, dst) in zip(loads[1:], pieces[1:]):
        load.wait()
        store(mid, dst)
    loads[0].wait()
    out_pb[...] = small[part_h : part_h + 1, :part1]
    low, high = small[:part_h, :64], small[:part_h, 64:]
    channels = jnp.concatenate([low, high, jnp.zeros((128 - part0, 64), F32)], axis=0)
    turned[...] = jnp.concatenate([channels, channels], axis=1).T
    for letter in range(4):
        out_ew[:, letter, :] = turned[16 * letter : 16 * letter + kernel_width, :part0]
    out_eb[...] = turned[15:16, :part0]
    out_gain[...] = turned[31:32, :part0]
    store(out_pb, gpb)
    store(out_ew, gew)
    store(out_eb, geb)
    store(out_gain, ggain)
    for copy in stores:
        copy.wait()


def shape(dims, kind):
    return jax.ShapeDtypeStruct(dims, kind)


def fused(bases, embed_weight, embed_bias, norm_gain, proj_weight, proj_bias, cotangent):
    kernel_width = embed_weight.shape[0]
    length = bases.shape[1]
    half = length // 2
    part0, d1 = proj_weight.shape
    part1 = proj_bias.shape[0]
    dp, seq = 8, 4
    d0, part_h = part0 * dp, part0 // 2
    big = half // 3
    vmem, hbm = pl.BlockSpec(memory_space=pltpu.VMEM), pl.BlockSpec(memory_space=pl.ANY)
    dma = pltpu.SemaphoreType.DMA
    scratch = [
        ((half, d1), BF16),
        ((1, length), jnp.int32),
        (embed_weight.shape, BF16),
        ((1, part0), BF16),
        ((1, part0), BF16),
        ((1, part1), BF16),
        ((2, 128), jnp.int32),
        ((16, length), jnp.int32),
        ((length, 128), F32),
        ((2, half, 64), BF16),
        ((2, big, d0), F32),
        ((2, half, d0), F32),
        ((2, half, d0), F32),
        ((2, half, 128), F32),
        ((half, d0), BF16),
        ((2, half, d0), BF16),
        ((2, big, d0), F32),
        ((8, d0), F32),
        ((128, 128), F32),
        ((part_h + 16, 128), BF16),
        ((dp, part_h + 16, 128), BF16),
        ((dp, 2, part_h, d1), BF16),
        ((half, d1), BF16),
        ((dp, 2, part_h, d1), BF16),
        ((2, 4, part_h, d1), BF16),
        ((2, 4, part_h, d1), BF16),
        ((2, 4, part_h, d1), BF16),
        ((2, part_h, d1), BF16),
        ((4, part_h, d1), BF16),
        ((2, part_h, d1), BF16),
        ((dp, part_h + 16, 128), BF16),
        ((dp, part_h + 16, 128), BF16),
        ((seq, part_h + 16, 128), BF16),
    ]
    pooled, gw, small = pl.pallas_call(
        functools.partial(fused_kernel, kernel_width),
        out_shape=(
            shape((half, d1), BF16), shape((part0, d1), F32), shape((part_h + 16, 128), F32)
        ),
        in_specs=[hbm] * 7,
        out_specs=(hbm, vmem, vmem),
        scratch_shapes=[pltpu.VMEM(dims, kind) for dims, kind in scratch]
        + [dma((n,)) for n in (96, 2, dp)]
        + [dma((dp, 2)), dma((2,)), dma((2, 4)), dma((4,)), dma((2,)), dma((dp,)), dma((seq,)), dma((9,))],
        compiler_params=pltpu.CompilerParams(
            collective_id=0, has_side_effects=True, vmem_limit_bytes=60 * 2**20
        ),
        name="fused_step",
    )(
        bases, embed_weight, embed_bias[None], norm_gain[None], proj_weight, proj_bias[None],
        cotangent[0],
    )
    outs = pl.pallas_call(
        functools.partial(finish_kernel, kernel_width),
        out_shape=(
            shape((half, d1), BF16),
            shape(embed_weight.shape, F32),
            shape((1, part0), F32),
            shape((1, part0), F32),
            shape((part0, d1), F32),
            shape((1, part1), F32),
        ),
        in_specs=[hbm] * 3,
        out_specs=(hbm,) * 6,
        scratch_shapes=[
            pltpu.VMEM((128, 128), F32),
            pltpu.VMEM((half, d1), BF16),
            pltpu.VMEM((part0, d1), F32),
            pltpu.VMEM((part_h + 16, 128), F32),
            pltpu.VMEM(embed_weight.shape, F32),
            pltpu.VMEM((1, part0), F32),
            pltpu.VMEM((1, part0), F32),
            pltpu.VMEM((1, part1), F32),
            dma((PIECES + 2,)),
            dma((PIECES + 5,)),
        ],
        compiler_params=pltpu.CompilerParams(vmem_limit_bytes=60 * 2**20),
        name="finish_step",
    )(pooled, gw, small)
    return (outs[0][None], outs[1], outs[2][0], outs[3][0], outs[4], outs[5][0])


def with_halo(x, sides, width):
    for axis, dim in sides:
        devices, length = (lax.axis_size(axis), x.shape[dim])
        up = [(i, (i + 1) % devices) for i in range(devices - 1)]
        down = [(j, i) for i, j in up]
        last = lax.slice_in_dim(x, length - width, length, axis=dim)
        leading = lax.slice_in_dim(x, 0, width, axis=dim)
        before = lax.ppermute(last, axis, up)
        after = lax.ppermute(leading, axis, down)
        x = jnp.concatenate([before, x, after], axis=dim)
    return x


def plain(bases, embed_weight, embed_bias, norm_gain, proj_weight, proj_bias, cotangent):
    kernel_width = embed_weight.shape[0]
    row_count = bases.shape[1]
    codes = bases + 1
    padded = with_halo(codes, (("seq", 1),), kernel_width // 2)[0]
    full_embed, full_bias, full_gain, full_proj, full_proj_bias = (
        lax.all_gather(embed_weight, "dp", axis=2, tiled=True),
        lax.all_gather(embed_bias, "dp", axis=0, tiled=True),
        lax.all_gather(norm_gain, "dp", axis=0, tiled=True),
        lax.all_gather(proj_weight, "dp", axis=0, tiled=True),
        lax.all_gather(proj_bias, "dp", axis=0, tiled=True),
    )
    letters = jnp.arange(1, 5, dtype=jnp.int32)
    features = jnp.concatenate(
        [
            (padded[k : k + row_count, None] == letters).astype(jnp.bfloat16)
            for k in range(kernel_width)
        ],
        axis=1,
    )
    flat_weight = full_embed.reshape(kernel_width * 4, -1)
    embedded = (
        jnp.dot(features, flat_weight, preferred_element_type=jnp.float32)
        + full_bias.astype(jnp.float32)
    ).astype(jnp.bfloat16)
    values = embedded.astype(jnp.float32)
    inverse = lax.rsqrt(jnp.mean(values * values, axis=1, keepdims=True) + 1e-06)
    scaled = values * inverse
    normed = scaled * full_gain.astype(jnp.float32)
    activated = jax.nn.gelu(normed, approximate=True).astype(jnp.bfloat16)
    product = jnp.dot(activated, full_proj, preferred_element_type=jnp.float32)
    mixed = product + full_proj_bias.astype(jnp.float32)
    pooled = jnp.mean(mixed.reshape(row_count // 2, 2, -1), axis=1).astype(jnp.bfloat16)
    scale_factor = 0.5 / (row_count * lax.axis_size("seq") * lax.axis_size("dp"))
    grad_mixed = (jnp.repeat(cotangent[0].astype(jnp.float32), 2, axis=0) * scale_factor).astype(
        jnp.bfloat16
    )
    grad_proj_weight = lax.dot_general(
        activated, grad_mixed, (((0,), (0,)), ((), ())), preferred_element_type=jnp.float32
    )
    grad_proj_bias = jnp.sum(grad_mixed.astype(jnp.float32), axis=0)
    grad_activated = lax.dot_general(
        grad_mixed, full_proj, (((1,), (1,)), ((), ())), preferred_element_type=jnp.float32
    )
    _, pullback = jax.vjp(lambda v: jax.nn.gelu(v, approximate=True), normed)
    grad_normed = pullback(grad_activated)[0]
    grad_norm_gain = jnp.sum(grad_normed * scaled, axis=0)
    weighted = grad_normed * full_gain.astype(jnp.float32)
    grad_embedded = (
        inverse * (weighted - scaled * jnp.mean(weighted * scaled, axis=1, keepdims=True))
    ).astype(jnp.bfloat16)
    grad_embed_weight = lax.dot_general(
        features, grad_embedded, (((0,), (0,)), ((), ())), preferred_element_type=jnp.float32
    ).reshape(kernel_width, 4, -1)
    grad_embed_bias = jnp.sum(grad_embedded.astype(jnp.float32), axis=0)
    whole = lax.psum(
        (grad_embed_weight, grad_embed_bias, grad_norm_gain, grad_proj_weight, grad_proj_bias),
        "seq",
    )
    results = (
        lax.psum_scatter(whole[0], "dp", scatter_dimension=2, tiled=True),
        lax.psum_scatter(whole[1], "dp", scatter_dimension=0, tiled=True),
        lax.psum_scatter(whole[2], "dp", scatter_dimension=0, tiled=True),
        lax.psum_scatter(whole[3], "dp", scatter_dimension=0, tiled=True),
        lax.psum_scatter(whole[4], "dp", scatter_dimension=0, tiled=True),
    )
    return (pooled[None], results[0], results[1], results[2], results[3], results[4])


def solution(mesh):
    placed = (
        P("dp", "seq"),
        P(None, None, "dp"),
        P("dp"),
        P("dp"),
        P("dp", None),
        P("dp"),
        P("dp", "seq", None),
    )
    step = fused if (mesh.shape["dp"], mesh.shape["seq"]) == (8, 4) else plain
    return jax.shard_map(
        step,
        mesh=mesh,
        in_specs=placed,
        out_specs=(
            P("dp", "seq", None),
            P(None, None, "dp"),
            P("dp"),
            P("dp"),
            P("dp", None),
            P("dp"),
        ),
        check_vma=False,
    )
```

```python
import functools

import jax
import jax.numpy as jnp
from jax import lax
from jax.experimental import pallas as pl
from jax.experimental.pallas import tpu as pltpu
from jax.sharding import PartitionSpec as P

F32, BF16 = jnp.float32, jnp.bfloat16
CUBIC = 0.044715
ROOT = 0.7978845608028654
NN = (((1,), (0,)), ((), ()))
NT = (((1,), (1,)), ((), ()))
TN = (((0,), (0,)), ((), ()))
MESH = pl.DeviceIdType.MESH
STEP = 16
PIECES = 4


def dot(a, b, dims):
    return lax.dot_general(a, b, dims, preferred_element_type=F32)


def build_features(bases_ref, halo_ref, stack_ref, wide_ref, feat_ref, kernel_width):
    length = bases_ref.shape[1]
    half, total = length // 2, length + 256
    ext = jnp.concatenate([halo_ref[0:1], bases_ref[...] + 1, halo_ref[1:2]], axis=1)
    ext = jnp.broadcast_to(ext, (8, total))
    for k in range(kernel_width):
        shift = k - kernel_width // 2
        moved = ext if shift == 0 else pltpu.roll(ext, (-shift) % total, 1)
        stack_ref[k : k + 1, :] = moved[0:1, 128 : 128 + length]
    stack_ref[kernel_width : kernel_width + 1, :] = jnp.ones((1, length), jnp.int32)
    stack = stack_ref[...]
    hot = jnp.concatenate([jnp.where(stack == c + 1, 1.0, 0.0) for c in range(4)] * 2, axis=0)
    wide_ref[...] = hot.T
    for parity in range(2):
        feat_ref[parity] = wide_ref[pl.ds(parity, half, stride=2), :][:, :64].astype(BF16)


def wide(lanes, width):
    return jnp.concatenate([lanes] * (width // 128), axis=1)


def forward_chunk(start, size, feat_ref, weight, gain, emb_ref, scaled_ref, slope_ref, inv_ref, pact_ref):
    width = gain.shape[1]
    for parity in range(2):
        emb = dot(feat_ref[parity, start : start + size, :], weight, NT)
        emb = emb.astype(BF16).astype(F32)
        emb_ref[parity] = emb
        inverse = lax.rsqrt(jnp.sum(emb * emb, axis=1, keepdims=True) * (1.0 / width) + 1e-6)
        inv_ref[parity, start : start + size, :] = jnp.broadcast_to(inverse, (size, 128))
    for r in range(0, size, STEP):
        rows = slice(start + r, start + r + STEP)
        total = None
        for parity in range(2):
            scaled = emb_ref[parity, r : r + STEP, :] * wide(inv_ref[parity, rows, :], width)
            x = scaled * gain
            sq = x * x
            t = 0.5 + 0.5 * jnp.tanh(x * (ROOT + (ROOT * CUBIC) * sq))
            act = x * t
            slope = t + act * (1.0 - t) * (2.0 * ROOT + (6.0 * ROOT * CUBIC) * sq)
            scaled_ref[parity, rows, :] = scaled
            slope_ref[parity, rows, :] = slope
            total = act if total is None else total + act
        pact_ref[rows, :] = total.astype(BF16)


def backward_chunk(
    start, size, cot_ref, w, gain, ga_ref, mean_ref, scaled_ref, slope_ref, inv_ref, ge_ref, acc_ref
):
    ga_ref[...] = dot(cot_ref[start : start + size, :], w, NT)
    width = ga_ref.shape[1]
    acc = acc_ref[...]
    for r in range(0, size, STEP):
        rows = slice(start + r, start + r + STEP)
        ga = ga_ref[r : r + STEP, :]
        for parity in range(2):
            q = ga * slope_ref[parity, rows, :] * scaled_ref[parity, rows, :]
            acc = acc + (q[:8] + q[8:])
            mean = jnp.sum(q * gain, axis=1, keepdims=True) * (1.0 / width)
            mean_ref[parity, r : r + STEP, :] = jnp.broadcast_to(mean, (STEP, 128))
    acc_ref[...] = acc
    for r in range(0, size, STEP):
        rows = slice(start + r, start + r + STEP)
        back = ga_ref[r : r + STEP, :] * gain
        for parity in range(2):
            mean = wide(mean_ref[parity, r : r + STEP, :], width)
            inverse = wide(inv_ref[parity, rows, :], width)
            ge = inverse * (back * slope_ref[parity, rows, :] - scaled_ref[parity, rows, :] * mean)
            ge_ref[parity, rows, :] = ge.astype(BF16)


def fused_kernel(
    kernel_width,
    bases_hbm, ew_hbm, eb_hbm, gain_hbm, w_hbm, pb_hbm, cot_hbm,
    pooled_hbm, gw_ref, small_out,
    pooled, bases, ew, eb, gain_in, pb, halo, stack, turned_feat, feat, emb, scaled, slope, inv, pact, ge, ga, mean, acc,
    rows_in, pack, packs, wbuf, cot, gwb, s1buf, p1, s2buf, sum2, s3buf, fin, small, sbuf, tbuf,
    send_sem, halo_recv, pack_recv, w_recv, s1_recv, s2_recv, s3_recv, fin_recv,
    small_recv, t_recv, local_sem,
):
    dp, seq = 8, 4
    length = bases.shape[1]
    half = length // 2
    part0, d1 = w_hbm.shape
    d0, part1, part_h = part0 * dp, d1 // dp, part0 // 2
    me, pos = lax.axis_index("dp"), lax.axis_index("seq")
    z, y, x, c = me // 2, me % 2, pos // 2, pos % 2
    y2, x2, c2 = 1 - y, 1 - x, 1 - c
    mate, across, skew = 2 * x + c2, 2 * x2 + c, 2 * x2 + c2
    own_rank = z % 2 == x
    factor = 0.25 / (half * seq * dp)

    barrier = pltpu.get_barrier_semaphore()
    for j in range(1, dp):
        pl.semaphore_signal(
            barrier, inc=1, device_id={"dp": (me + j) % dp, "seq": pos}, device_id_type=MESH
        )
    for j in range(1, seq):
        for to in (me, 2 * z + y2):
            pl.semaphore_signal(
                barrier, inc=1, device_id={"dp": to, "seq": (pos + j) % seq}, device_id_type=MESH
            )

    loads = [
        pltpu.make_async_copy(src, dst, local_sem.at[i])
        for i, (src, dst) in enumerate(
            [
                (ew_hbm, ew), (eb_hbm, eb), (gain_hbm, gain_in), (pb_hbm, pb), (bases_hbm, bases),
                (w_hbm.at[:part_h], wbuf.at[me, 0]), (w_hbm.at[part_h:], wbuf.at[me, 1]),
                (cot_hbm, cot),
            ]
        )
    ]
    for load in loads:
        load.start()
    rows_in[...] = jnp.zeros_like(rows_in)
    acc[...] = jnp.zeros_like(acc)
    for load in loads[:4]:
        load.wait()
    values = ew[...].astype(F32)
    for letter in range(4):
        rows_in[16 * letter : 16 * letter + kernel_width, :part0] = values[:, letter, :]
    rows_in[15:16, :part0] = eb[...].astype(F32)
    rows_in[31:32, :part0] = gain_in[...].astype(F32)
    turned = rows_in[...].T
    pack[:part_h, :] = jnp.concatenate(
        [turned[:part_h, :64], turned[part_h:part0, :64]], axis=1
    ).astype(BF16)
    tail = jnp.concatenate([pb[...].astype(F32), jnp.zeros((1, 128 - part1), F32)], axis=1)
    pack[part_h:, :] = jnp.broadcast_to(tail, (16, 128)).astype(BF16)
    packs[me] = pack[...]
    for load in loads[4:7]:
        load.wait()

    pl.semaphore_wait(barrier, dp - 1 + 2 * (seq - 1))

    started = []

    def send(src, dst, recv, to_dp, to_seq, pred=None):
        copy = pltpu.make_async_remote_copy(
            src_ref=src, dst_ref=dst, send_sem=send_sem.at[len(started)], recv_sem=recv,
            device_id={"dp": to_dp, "seq": to_seq}, device_id_type=MESH,
        )
        started.append((copy, pred))
        if pred is None:
            copy.start()
        else:
            pl.when(pred)(lambda: copy.start())

    def arrive(dst, recv, pred=None):
        copy = pltpu.make_async_remote_copy(
            src_ref=dst, dst_ref=dst, send_sem=send_sem.at[0], recv_sem=recv,
            device_id={"dp": me, "seq": mate}, device_id_type=MESH,
        )
        if pred is None:
            copy.wait_recv()
        else:
            pl.when(pred)(lambda: copy.wait_recv())

    send(bases.at[:, length - 128 :], halo.at[0:1], halo_recv.at[0], me, pos + 1, pos < seq - 1)
    send(bases.at[:, :128], halo.at[1:2], halo_recv.at[1], me, pos - 1, pos > 0)
    for j in range(1, dp):
        send(pack, packs.at[me], pack_recv.at[me], (me + j) % dp, pos)
    send(wbuf.at[me, c], wbuf.at[me, c], w_recv.at[me, c], 2 * z + y2, pos)

    def shard_out(distances):
        for zz in range(4):
            for distance in distances:
                there = (z == zz - distance) | (z == zz + distance)
                send(wbuf.at[me, c], wbuf.at[me, c], w_recv.at[me, c], 2 * zz + y, pos, there)

    shard_out((1,))

    arrive(halo.at[0:1], halo_recv.at[0], pos > 0)
    arrive(halo.at[1:2], halo_recv.at[1], pos < seq - 1)
    for side, edge in ((0, 0), (1, seq - 1)):

        @pl.when(pos == edge)
        def _(side=side):
            halo[side : side + 1, :] = jnp.zeros((1, 128), jnp.int32)

        @pl.when(pos != edge)
        def _(side=side):
            halo[side : side + 1, :] = halo[side : side + 1, :] + 1


    build_features(bases, halo, stack, turned_feat, feat, kernel_width)
    for j in range(1, dp):
        arrive(packs.at[(me + j) % dp], pack_recv.at[(me + j) % dp])
    shard_out((3, 2))
    weight = jnp.concatenate(
        [packs[d, :part_h, 64 * h : 64 * h + 64] for d in range(dp) for h in range(2)], axis=0
    )
    lanes = lax.broadcasted_iota(jnp.int32, (16, 64), 1)
    gain = dot(jnp.where(lanes == 31, 1.0, 0.0).astype(BF16), weight, NT)[0:1]
    size = half // 3

    def forward(i):
        forward_chunk(i * size, size, feat, weight, gain, emb.at[i % 2], scaled, slope, inv, pact)

    def relay(distances):
        for zz in range(4):
            d = 2 * zz + y
            slot, sem = wbuf.at[d, c], w_recv.at[d, c]
            for distance in distances:
                there = (z == zz - distance) | (z == zz + distance)
                arrive(slot, sem, there)
                send(slot, slot, sem, 2 * z + y2, pos, there)
                send(slot, slot, sem, me, mate, there)

    forward(0)
    relay((1,))
    d = 2 * z + y2
    arrive(wbuf.at[d, c], w_recv.at[d, c])
    send(wbuf.at[d, c], wbuf.at[d, c], w_recv.at[d, c], me, mate)
    forward(1)
    forward(2)

    loads[7].wait()
    block = d0 // 2
    for b in range(2):
        value = dot(pact[:, b * block : (b + 1) * block], cot[...], TN)
        gwb[4 * b : 4 * b + 4] = value.astype(BF16).reshape(4, 2, part_h, d1)
        send(gwb.at[4 * b : 4 * b + 4, c2], s1buf.at[b], s1_recv.at[b], me, mate)
        if b == 0:
            relay((2, 3))

    rank = 2 * x + y
    others = (
        (2 * x2 + y2, 2 * z + y2, across),
        (2 * x + y2, 2 * z + y2, pos),
        (2 * x2 + y, me, across),
    )
    for b in range(2):
        arrive(s1buf.at[b], s1_recv.at[b])
        for k in range(4):
            p1[b, k] = (gwb[4 * b + k, c].astype(F32) + s1buf[b, k].astype(F32)).astype(BF16)
        for piece, to_dp, to_seq in others:
            send(p1.at[b, piece], s2buf.at[b, rank], s2_recv.at[b, rank], to_dp, to_seq)

    for zz in range(4):
        d = 2 * zz + y2
        slot, sem = wbuf.at[d, c], w_recv.at[d, c]
        arrive(slot, sem, z != zz)
        send(slot, slot, sem, me, mate, z != zz)

    for d in range(dp):
        arrive(wbuf.at[d, c2], w_recv.at[d, c2], me != d)

    tails = [packs[d, part_h:, :].astype(F32)[:8, :part1] for d in range(dp)]
    bias = jnp.concatenate(tails, axis=1)[0:1]

    big = half // 3
    for i in range(3):
        w = wbuf[...].reshape(d0, d1)
        value = 0.5 * dot(pact[i * big : (i + 1) * big, :], w, NN) + bias
        pooled[i * big : (i + 1) * big, :] = value.astype(BF16)
    pooled_out = pltpu.make_async_copy(pooled, pooled_hbm, local_sem.at[8])
    pooled_out.start()

    def backward(i):
        w = wbuf[...].reshape(d0, d1)
        backward_chunk(i * big, big, cot, w, gain, ga.at[i % 2], mean.at[i % 2], scaled, slope, inv, ge, acc)

    def plane_sum(k):
        total = p1[k, rank].astype(F32)
        for piece, _, _ in others:
            arrive(s2buf.at[k, piece], s2_recv.at[k, piece])
            total = total + s2buf[k, piece].astype(F32)
        sum2[k] = total.astype(BF16)
        zt = x + 2 * k
        send(sum2.at[k], s3buf.at[z], s3_recv.at[z], 2 * zt + y, pos, zt != z)

    backward(0)
    backward(1)
    plane_sum(0)
    backward(2)

    g = dot(feat[0], ge[0], TN) + dot(feat[1], ge[1], TN)
    gain_row = jnp.sum(acc[...], axis=0, keepdims=True)
    g = jnp.where(lax.broadcasted_iota(jnp.int32, (64, d0), 0) == 31, gain_row, g)
    turned = jnp.concatenate([g, jnp.zeros_like(g)], axis=0).T
    for d in range(dp):
        low = turned[d * part0 : d * part0 + part_h, :64]
        high = turned[d * part0 + part_h : (d + 1) * part0, :64]
        small[d, :part_h, :] = jnp.concatenate([low, high], axis=1).astype(BF16)
    sums = 2.0 * dot(jnp.ones((16, half), BF16), cot[...], NN)[0:8]
    for d in range(dp):
        own = jnp.concatenate(
            [sums[:, d * part1 : (d + 1) * part1], jnp.zeros((8, 128 - part1), F32)], axis=1
        )
        small[d, part_h:, :] = jnp.concatenate([own, own], axis=0).astype(BF16)
    for j in range(1, dp):
        to = (me + j) % dp
        send(small.at[to], sbuf.at[me], small_recv.at[me], to, pos)
    sbuf[me] = small[me]
    plane_sum(1)

    for zz in range(4):
        arrive(s3buf.at[zz], s3_recv.at[zz], own_rank & (z != zz))

    @pl.when(own_rank)
    def _():
        value = sum2[z // 2].astype(F32)
        for j in range(1, 4):
            value = value + s3buf[(z + j) % 4].astype(F32)
        fin[c] = value.astype(BF16)

    send(fin.at[c], fin.at[c], fin_recv.at[c], me, across, own_rank)
    arrive(fin.at[c], fin_recv.at[c], jnp.logical_not(own_rank))
    send(fin.at[c], fin.at[c], fin_recv.at[c], me, mate)

    for j in range(1, dp):
        arrive(sbuf.at[(me + j) % dp], small_recv.at[(me + j) % dp])
    tbuf[pos] = jnp.sum(sbuf[...].astype(F32), axis=0).astype(BF16)
    for j in range(1, seq):
        send(tbuf.at[pos], tbuf.at[pos], t_recv.at[pos], me, (pos + j) % seq)

    arrive(fin.at[c2], fin_recv.at[c2])
    gw_ref[...] = fin[...].astype(F32).reshape(part0, d1) * factor
    for j in range(1, seq):
        arrive(tbuf.at[(pos + j) % seq], t_recv.at[(pos + j) % seq])
    small_out[...] = jnp.sum(tbuf[...].astype(F32), axis=0) * factor

    for copy, pred in started:
        if pred is None:
            copy.wait_send()
        else:
            pl.when(pred)(lambda copy=copy: copy.wait_send())
    pooled_out.wait()


def finish_kernel(
    kernel_width, pooled_in, gw_in, small_in, pooled, gew, geb, ggain, gw, gpb,
    turned, held, held_gw, small, out_ew, out_eb, out_gain, out_pb, load_sem, store_sem,
):
    part0, part1 = gw_in.shape[0], gpb.shape[1]
    part_h = part0 // 2
    rows = pooled_in.shape[0] // PIECES
    pieces = [(small_in, small, None), (gw_in, held_gw, gw)]
    for i in range(PIECES):
        span = pl.ds(i * rows, rows)
        pieces.append((pooled_in.at[span], held.at[span], pooled.at[span]))
    loads = [
        pltpu.make_async_copy(src, mid, load_sem.at[i]) for i, (src, mid, _) in enumerate(pieces)
    ]
    for load in loads:
        load.start()
    stores = []

    def store(src, dst):
        copy = pltpu.make_async_copy(src, dst, store_sem.at[len(stores)])
        stores.append(copy)
        copy.start()

    for load, (_, mid, dst) in zip(loads[1:], pieces[1:]):
        load.wait()
        store(mid, dst)
    loads[0].wait()
    out_pb[...] = small[part_h : part_h + 1, :part1]
    low, high = small[:part_h, :64], small[:part_h, 64:]
    channels = jnp.concatenate([low, high, jnp.zeros((128 - part0, 64), F32)], axis=0)
    turned[...] = jnp.concatenate([channels, channels], axis=1).T
    for letter in range(4):
        out_ew[:, letter, :] = turned[16 * letter : 16 * letter + kernel_width, :part0]
    out_eb[...] = turned[15:16, :part0]
    out_gain[...] = turned[31:32, :part0]
    store(out_pb, gpb)
    store(out_ew, gew)
    store(out_eb, geb)
    store(out_gain, ggain)
    for copy in stores:
        copy.wait()


def shape(dims, kind):
    return jax.ShapeDtypeStruct(dims, kind)


def fused(bases, embed_weight, embed_bias, norm_gain, proj_weight, proj_bias, cotangent):
    kernel_width = embed_weight.shape[0]
    length = bases.shape[1]
    half = length // 2
    part0, d1 = proj_weight.shape
    part1 = proj_bias.shape[0]
    dp, seq = 8, 4
    d0, part_h = part0 * dp, part0 // 2
    big = half // 3
    vmem, hbm = pl.BlockSpec(memory_space=pltpu.VMEM), pl.BlockSpec(memory_space=pl.ANY)
    dma = pltpu.SemaphoreType.DMA
    scratch = [
        ((half, d1), BF16),
        ((1, length), jnp.int32),
        (embed_weight.shape, BF16),
        ((1, part0), BF16),
        ((1, part0), BF16),
        ((1, part1), BF16),
        ((2, 128), jnp.int32),
        ((16, length), jnp.int32),
        ((length, 128), F32),
        ((2, half, 64), BF16),
        ((2, 2, big, d0), F32),
        ((2, half, d0), F32),
        ((2, half, d0), F32),
        ((2, half, 128), F32),
        ((half, d0), BF16),
        ((2, half, d0), BF16),
        ((2, big, d0), F32),
        ((2, 2, big, 128), F32),
        ((8, d0), F32),
        ((128, 128), F32),
        ((part_h + 16, 128), BF16),
        ((dp, part_h + 16, 128), BF16),
        ((dp, 2, part_h, d1), BF16),
        ((half, d1), BF16),
        ((dp, 2, part_h, d1), BF16),
        ((2, 4, part_h, d1), BF16),
        ((2, 4, part_h, d1), BF16),
        ((2, 4, part_h, d1), BF16),
        ((2, part_h, d1), BF16),
        ((4, part_h, d1), BF16),
        ((2, part_h, d1), BF16),
        ((dp, part_h + 16, 128), BF16),
        ((dp, part_h + 16, 128), BF16),
        ((seq, part_h + 16, 128), BF16),
    ]
    pooled, gw, small = pl.pallas_call(
        functools.partial(fused_kernel, kernel_width),
        out_shape=(
            shape((half, d1), BF16), shape((part0, d1), F32), shape((part_h + 16, 128), F32)
        ),
        in_specs=[hbm] * 7,
        out_specs=(hbm, vmem, vmem),
        scratch_shapes=[pltpu.VMEM(dims, kind) for dims, kind in scratch]
        + [dma((n,)) for n in (96, 2, dp)]
        + [dma((dp, 2)), dma((2,)), dma((2, 4)), dma((4,)), dma((2,)), dma((dp,)), dma((seq,)), dma((9,))],
        compiler_params=pltpu.CompilerParams(
            collective_id=0, has_side_effects=True, vmem_limit_bytes=60 * 2**20
        ),
        name="fused_step",
    )(
        bases, embed_weight, embed_bias[None], norm_gain[None], proj_weight, proj_bias[None],
        cotangent[0],
    )
    outs = pl.pallas_call(
        functools.partial(finish_kernel, kernel_width),
        out_shape=(
            shape((half, d1), BF16),
            shape(embed_weight.shape, F32),
            shape((1, part0), F32),
            shape((1, part0), F32),
            shape((part0, d1), F32),
            shape((1, part1), F32),
        ),
        in_specs=[hbm] * 3,
        out_specs=(hbm,) * 6,
        scratch_shapes=[
            pltpu.VMEM((128, 128), F32),
            pltpu.VMEM((half, d1), BF16),
            pltpu.VMEM((part0, d1), F32),
            pltpu.VMEM((part_h + 16, 128), F32),
            pltpu.VMEM(embed_weight.shape, F32),
            pltpu.VMEM((1, part0), F32),
            pltpu.VMEM((1, part0), F32),
            pltpu.VMEM((1, part1), F32),
            dma((PIECES + 2,)),
            dma((PIECES + 5,)),
        ],
        compiler_params=pltpu.CompilerParams(vmem_limit_bytes=60 * 2**20),
        name="finish_step",
    )(pooled, gw, small)
    return (outs[0][None], outs[1], outs[2][0], outs[3][0], outs[4], outs[5][0])


def with_halo(x, sides, width):
    for axis, dim in sides:
        devices, length = (lax.axis_size(axis), x.shape[dim])
        up = [(i, (i + 1) % devices) for i in range(devices - 1)]
        down = [(j, i) for i, j in up]
        last = lax.slice_in_dim(x, length - width, length, axis=dim)
        leading = lax.slice_in_dim(x, 0, width, axis=dim)
        before = lax.ppermute(last, axis, up)
        after = lax.ppermute(leading, axis, down)
        x = jnp.concatenate([before, x, after], axis=dim)
    return x


def plain(bases, embed_weight, embed_bias, norm_gain, proj_weight, proj_bias, cotangent):
    kernel_width = embed_weight.shape[0]
    row_count = bases.shape[1]
    codes = bases + 1
    padded = with_halo(codes, (("seq", 1),), kernel_width // 2)[0]
    full_embed, full_bias, full_gain, full_proj, full_proj_bias = (
        lax.all_gather(embed_weight, "dp", axis=2, tiled=True),
        lax.all_gather(embed_bias, "dp", axis=0, tiled=True),
        lax.all_gather(norm_gain, "dp", axis=0, tiled=True),
        lax.all_gather(proj_weight, "dp", axis=0, tiled=True),
        lax.all_gather(proj_bias, "dp", axis=0, tiled=True),
    )
    letters = jnp.arange(1, 5, dtype=jnp.int32)
    features = jnp.concatenate(
        [
            (padded[k : k + row_count, None] == letters).astype(jnp.bfloat16)
            for k in range(kernel_width)
        ],
        axis=1,
    )
    flat_weight = full_embed.reshape(kernel_width * 4, -1)
    embedded = (
        jnp.dot(features, flat_weight, preferred_element_type=jnp.float32)
        + full_bias.astype(jnp.float32)
    ).astype(jnp.bfloat16)
    values = embedded.astype(jnp.float32)
    inverse = lax.rsqrt(jnp.mean(values * values, axis=1, keepdims=True) + 1e-06)
    scaled = values * inverse
    normed = scaled * full_gain.astype(jnp.float32)
    activated = jax.nn.gelu(normed, approximate=True).astype(jnp.bfloat16)
    product = jnp.dot(activated, full_proj, preferred_element_type=jnp.float32)
    mixed = product + full_proj_bias.astype(jnp.float32)
    pooled = jnp.mean(mixed.reshape(row_count // 2, 2, -1), axis=1).astype(jnp.bfloat16)
    scale_factor = 0.5 / (row_count * lax.axis_size("seq") * lax.axis_size("dp"))
    grad_mixed = (jnp.repeat(cotangent[0].astype(jnp.float32), 2, axis=0) * scale_factor).astype(
        jnp.bfloat16
    )
    grad_proj_weight = lax.dot_general(
        activated, grad_mixed, (((0,), (0,)), ((), ())), preferred_element_type=jnp.float32
    )
    grad_proj_bias = jnp.sum(grad_mixed.astype(jnp.float32), axis=0)
    grad_activated = lax.dot_general(
        grad_mixed, full_proj, (((1,), (1,)), ((), ())), preferred_element_type=jnp.float32
    )
    _, pullback = jax.vjp(lambda v: jax.nn.gelu(v, approximate=True), normed)
    grad_normed = pullback(grad_activated)[0]
    grad_norm_gain = jnp.sum(grad_normed * scaled, axis=0)
    weighted = grad_normed * full_gain.astype(jnp.float32)
    grad_embedded = (
        inverse * (weighted - scaled * jnp.mean(weighted * scaled, axis=1, keepdims=True))
    ).astype(jnp.bfloat16)
    grad_embed_weight = lax.dot_general(
        features, grad_embedded, (((0,), (0,)), ((), ())), preferred_element_type=jnp.float32
    ).reshape(kernel_width, 4, -1)
    grad_embed_bias = jnp.sum(grad_embedded.astype(jnp.float32), axis=0)
    whole = lax.psum(
        (grad_embed_weight, grad_embed_bias, grad_norm_gain, grad_proj_weight, grad_proj_bias),
        "seq",
    )
    results = (
        lax.psum_scatter(whole[0], "dp", scatter_dimension=2, tiled=True),
        lax.psum_scatter(whole[1], "dp", scatter_dimension=0, tiled=True),
        lax.psum_scatter(whole[2], "dp", scatter_dimension=0, tiled=True),
        lax.psum_scatter(whole[3], "dp", scatter_dimension=0, tiled=True),
        lax.psum_scatter(whole[4], "dp", scatter_dimension=0, tiled=True),
    )
    return (pooled[None], results[0], results[1], results[2], results[3], results[4])


def solution(mesh):
    placed = (
        P("dp", "seq"),
        P(None, None, "dp"),
        P("dp"),
        P("dp"),
        P("dp", None),
        P("dp"),
        P("dp", "seq", None),
    )
    step = fused if (mesh.shape["dp"], mesh.shape["seq"]) == (8, 4) else plain
    return jax.shard_map(
        step,
        mesh=mesh,
        in_specs=placed,
        out_specs=(
            P("dp", "seq", None),
            P(None, None, "dp"),
            P("dp"),
            P("dp"),
            P("dp", None),
            P("dp"),
        ),
        check_vma=False,
    )
```

```python
import functools

import jax
import jax.numpy as jnp
from jax import lax
from jax.experimental import pallas as pl
from jax.experimental.pallas import tpu as pltpu
from jax.sharding import PartitionSpec as P

F32, BF16 = jnp.float32, jnp.bfloat16
CUBIC = 0.044715
ROOT = 0.7978845608028654
NN = (((1,), (0,)), ((), ()))
NT = (((1,), (1,)), ((), ()))
TN = (((0,), (0,)), ((), ()))
MESH = pl.DeviceIdType.MESH
STEP = 16
PIECES = 4


def dot(a, b, dims):
    return lax.dot_general(a, b, dims, preferred_element_type=F32)


def build_features(bases_ref, halo_ref, stack_ref, wide_ref, feat_ref, kernel_width):
    length = bases_ref.shape[1]
    half, total = length // 2, length + 256
    ext = jnp.concatenate([halo_ref[0:1], bases_ref[...] + 1, halo_ref[1:2]], axis=1)
    ext = jnp.broadcast_to(ext, (8, total))
    for k in range(kernel_width):
        shift = k - kernel_width // 2
        moved = ext if shift == 0 else pltpu.roll(ext, (-shift) % total, 1)
        stack_ref[k : k + 1, :] = moved[0:1, 128 : 128 + length]
    stack_ref[kernel_width : kernel_width + 1, :] = jnp.ones((1, length), jnp.int32)
    stack = stack_ref[...]
    hot = jnp.concatenate([jnp.where(stack == c + 1, 1.0, 0.0) for c in range(4)] * 2, axis=0)
    wide_ref[...] = hot.T
    for parity in range(2):
        feat_ref[parity] = wide_ref[pl.ds(parity, half, stride=2), :][:, :64].astype(BF16)


def wide(lanes, width):
    return jnp.concatenate([lanes] * (width // 128), axis=1)


def forward_chunk(start, size, feat_ref, weight, gain, emb_ref, scaled_ref, slope_ref, inv_ref, pact_ref):
    width = gain.shape[1]
    for parity in range(2):
        emb = dot(feat_ref[parity, start : start + size, :], weight, NT)
        emb = emb.astype(BF16).astype(F32)
        emb_ref[parity] = emb
        inverse = lax.rsqrt(jnp.sum(emb * emb, axis=1, keepdims=True) * (1.0 / width) + 1e-6)
        inv_ref[parity, start : start + size, :] = jnp.broadcast_to(inverse, (size, 128))
    for r in range(0, size, STEP):
        rows = slice(start + r, start + r + STEP)
        total = None
        for parity in range(2):
            scaled = emb_ref[parity, r : r + STEP, :] * wide(inv_ref[parity, rows, :], width)
            x = scaled * gain
            sq = x * x
            t = 0.5 + 0.5 * jnp.tanh(x * (ROOT + (ROOT * CUBIC) * sq))
            act = x * t
            slope = t + act * (1.0 - t) * (2.0 * ROOT + (6.0 * ROOT * CUBIC) * sq)
            scaled_ref[parity, rows, :] = scaled
            slope_ref[parity, rows, :] = slope
            total = act if total is None else total + act
        pact_ref[rows, :] = total.astype(BF16)


def backward_chunk(
    start, size, cot_ref, w, gain, ga_ref, mean_ref, scaled_ref, slope_ref, inv_ref, ge_ref, acc_ref
):
    ga_ref[...] = dot(cot_ref[start : start + size, :], w, NT)
    width = ga_ref.shape[1]
    acc = acc_ref[...]
    for r in range(0, size, STEP):
        rows = slice(start + r, start + r + STEP)
        ga = ga_ref[r : r + STEP, :]
        for parity in range(2):
            q = ga * slope_ref[parity, rows, :] * scaled_ref[parity, rows, :]
            acc = acc + (q[:8] + q[8:])
            mean = jnp.sum(q * gain, axis=1, keepdims=True) * (1.0 / width)
            mean_ref[parity, r : r + STEP, :] = jnp.broadcast_to(mean, (STEP, 128))
    acc_ref[...] = acc
    for r in range(0, size, STEP):
        rows = slice(start + r, start + r + STEP)
        back = ga_ref[r : r + STEP, :] * gain
        for parity in range(2):
            mean = wide(mean_ref[parity, r : r + STEP, :], width)
            inverse = wide(inv_ref[parity, rows, :], width)
            ge = inverse * (back * slope_ref[parity, rows, :] - scaled_ref[parity, rows, :] * mean)
            ge_ref[parity, rows, :] = ge.astype(BF16)


def fused_kernel(
    kernel_width,
    bases_hbm, ew_hbm, eb_hbm, gain_hbm, w_hbm, pb_hbm, cot_hbm,
    pooled_hbm, gw_ref, small_out,
    pooled, bases, ew, eb, gain_in, pb, halo, stack, turned_feat, feat, emb, scaled, slope, inv, pact, ge, ga, mean, acc,
    rows_in, pack, packs, wbuf, cot, gwb, s1buf, p1, s2buf, sum2, s3buf, fin, small, sbuf, tbuf,
    send_sem, halo_recv, pack_recv, w_recv, s1_recv, s2_recv, s3_recv, fin_recv,
    small_recv, t_recv, local_sem,
):
    dp, seq = 8, 4
    length = bases.shape[1]
    half = length // 2
    part0, d1 = w_hbm.shape
    d0, part1, part_h = part0 * dp, d1 // dp, part0 // 2
    me, pos = lax.axis_index("dp"), lax.axis_index("seq")
    z, y, x, c = me // 2, me % 2, pos // 2, pos % 2
    y2, x2, c2 = 1 - y, 1 - x, 1 - c
    mate, across, skew = 2 * x + c2, 2 * x2 + c, 2 * x2 + c2
    own_rank = z % 2 == x
    factor = 0.25 / (half * seq * dp)

    barrier = pltpu.get_barrier_semaphore()
    for j in range(1, dp):
        pl.semaphore_signal(
            barrier, inc=1, device_id={"dp": (me + j) % dp, "seq": pos}, device_id_type=MESH
        )
    for j in range(1, seq):
        for to in (me, 2 * z + y2):
            pl.semaphore_signal(
                barrier, inc=1, device_id={"dp": to, "seq": (pos + j) % seq}, device_id_type=MESH
            )

    loads = [
        pltpu.make_async_copy(src, dst, local_sem.at[i])
        for i, (src, dst) in enumerate(
            [
                (ew_hbm, ew), (eb_hbm, eb), (gain_hbm, gain_in), (pb_hbm, pb), (bases_hbm, bases),
                (w_hbm.at[:part_h], wbuf.at[me, 0]), (w_hbm.at[part_h:], wbuf.at[me, 1]),
                (cot_hbm, cot),
            ]
        )
    ]
    for load in loads:
        load.start()
    rows_in[...] = jnp.zeros_like(rows_in)
    acc[...] = jnp.zeros_like(acc)
    for load in loads[:4]:
        load.wait()
    values = ew[...].astype(F32)
    for letter in range(4):
        rows_in[16 * letter : 16 * letter + kernel_width, :part0] = values[:, letter, :]
    rows_in[15:16, :part0] = eb[...].astype(F32)
    rows_in[31:32, :part0] = gain_in[...].astype(F32)
    turned = rows_in[...].T
    pack[:part_h, :] = jnp.concatenate(
        [turned[:part_h, :64], turned[part_h:part0, :64]], axis=1
    ).astype(BF16)
    tail = jnp.concatenate([pb[...].astype(F32), jnp.zeros((1, 128 - part1), F32)], axis=1)
    pack[part_h:, :] = jnp.broadcast_to(tail, (16, 128)).astype(BF16)
    packs[me] = pack[...]
    for load in loads[4:7]:
        load.wait()

    pl.semaphore_wait(barrier, dp - 1 + 2 * (seq - 1))

    started = []

    def send(src, dst, recv, to_dp, to_seq, pred=None):
        copy = pltpu.make_async_remote_copy(
            src_ref=src, dst_ref=dst, send_sem=send_sem.at[len(started)], recv_sem=recv,
            device_id={"dp": to_dp, "seq": to_seq}, device_id_type=MESH,
        )
        started.append((copy, pred))
        if pred is None:
            copy.start()
        else:
            pl.when(pred)(lambda: copy.start())

    def arrive(dst, recv, pred=None):
        copy = pltpu.make_async_remote_copy(
            src_ref=dst, dst_ref=dst, send_sem=send_sem.at[0], recv_sem=recv,
            device_id={"dp": me, "seq": mate}, device_id_type=MESH,
        )
        if pred is None:
            copy.wait_recv()
        else:
            pl.when(pred)(lambda: copy.wait_recv())

    send(bases.at[:, length - 128 :], halo.at[0:1], halo_recv.at[0], me, pos + 1, pos < seq - 1)
    send(bases.at[:, :128], halo.at[1:2], halo_recv.at[1], me, pos - 1, pos > 0)
    for j in range(1, dp):
        send(pack, packs.at[me], pack_recv.at[me], (me + j) % dp, pos)
    send(wbuf.at[me, c], wbuf.at[me, c], w_recv.at[me, c], 2 * z + y2, pos)

    def shard_out(distances):
        for zz in range(4):
            for distance in distances:
                there = (z == zz - distance) | (z == zz + distance)
                send(wbuf.at[me, c], wbuf.at[me, c], w_recv.at[me, c], 2 * zz + y, pos, there)

    shard_out((1,))

    arrive(halo.at[0:1], halo_recv.at[0], pos > 0)
    arrive(halo.at[1:2], halo_recv.at[1], pos < seq - 1)
    for side, edge in ((0, 0), (1, seq - 1)):

        @pl.when(pos == edge)
        def _(side=side):
            halo[side : side + 1, :] = jnp.zeros((1, 128), jnp.int32)

        @pl.when(pos != edge)
        def _(side=side):
            halo[side : side + 1, :] = halo[side : side + 1, :] + 1


    build_features(bases, halo, stack, turned_feat, feat, kernel_width)
    for j in range(1, dp):
        arrive(packs.at[(me + j) % dp], pack_recv.at[(me + j) % dp])
    shard_out((3, 2))
    weight = jnp.concatenate(
        [packs[d, :part_h, 64 * h : 64 * h + 64] for d in range(dp) for h in range(2)], axis=0
    )
    lanes = lax.broadcasted_iota(jnp.int32, (16, 64), 1)
    gain = dot(jnp.where(lanes == 31, 1.0, 0.0).astype(BF16), weight, NT)[0:1]
    size = half // 3

    def forward(i):
        forward_chunk(i * size, size, feat, weight, gain, emb.at[i % 2], scaled, slope, inv, pact)

    def relay(distances):
        for zz in range(4):
            d = 2 * zz + y
            slot, sem = wbuf.at[d, c], w_recv.at[d, c]
            for distance in distances:
                there = (z == zz - distance) | (z == zz + distance)
                arrive(slot, sem, there)
                send(slot, slot, sem, 2 * z + y2, pos, there)
                send(slot, slot, sem, me, mate, there)

    forward(0)
    relay((1,))
    d = 2 * z + y2
    arrive(wbuf.at[d, c], w_recv.at[d, c])
    send(wbuf.at[d, c], wbuf.at[d, c], w_recv.at[d, c], me, mate)
    forward(1)
    forward(2)

    loads[7].wait()
    block = d0 // 2
    for b in range(2):
        value = dot(pact[:, b * block : (b + 1) * block], cot[...], TN)
        gwb[4 * b : 4 * b + 4] = value.astype(BF16).reshape(4, 2, part_h, d1)
        send(gwb.at[4 * b : 4 * b + 4, c2], s1buf.at[b], s1_recv.at[b], me, mate)
        if b == 0:
            relay((2, 3))

    rank = 2 * x + y
    for b in range(2):
        arrive(s1buf.at[b], s1_recv.at[b])
        for k in range(4):
            p1[b, k] = (gwb[4 * b + k, c].astype(F32) + s1buf[b, k].astype(F32)).astype(BF16)
        if b == 0:
            send(p1.at[0, pl.ds(2 * x2, 2)], s2buf.at[0, 0:2], s2_recv.at[0, 0], me, across)
        else:
            for xx in range(2):
                send(p1.at[1, 2 * xx + y2], s2buf.at[1, xx], s2_recv.at[1, xx], 2 * z + y2, pos)

    for zz in range(4):
        d = 2 * zz + y2
        slot, sem = wbuf.at[d, c], w_recv.at[d, c]
        arrive(slot, sem, z != zz)
        send(slot, slot, sem, me, mate, z != zz)

    for d in range(dp):
        arrive(wbuf.at[d, c2], w_recv.at[d, c2], me != d)

    tails = [packs[d, part_h:, :].astype(F32)[:8, :part1] for d in range(dp)]
    bias = jnp.concatenate(tails, axis=1)[0:1]

    big = half // 3
    for i in range(3):
        w = wbuf[...].reshape(d0, d1)
        value = 0.5 * dot(pact[i * big : (i + 1) * big, :], w, NN) + bias
        pooled[i * big : (i + 1) * big, :] = value.astype(BF16)
    pooled_out = pltpu.make_async_copy(pooled, pooled_hbm, local_sem.at[8])
    pooled_out.start()

    def backward(i):
        w = wbuf[...].reshape(d0, d1)
        backward_chunk(i * big, big, cot, w, gain, ga.at[i % 2], mean.at[i % 2], scaled, slope, inv, ge, acc)

    def add(k, piece, arrived):
        p1[k, piece] = (p1[k, piece].astype(F32) + s2buf[k, arrived].astype(F32)).astype(BF16)

    def pair_sums():
        arrive(s2buf.at[0, 0:2], s2_recv.at[0, 0])
        for yy in range(2):
            add(0, 2 * x + yy, yy)
        send(p1.at[0, 2 * x + y2], s2buf.at[0, 2], s2_recv.at[0, 2], 2 * z + y2, pos)
        for xx in range(2):
            arrive(s2buf.at[1, xx], s2_recv.at[1, xx])
            add(1, 2 * xx + y, xx)
        send(p1.at[1, 2 * x2 + y], s2buf.at[1, 2], s2_recv.at[1, 2], me, across)

    def plane_sum(k):
        arrive(s2buf.at[k, 2], s2_recv.at[k, 2])
        total = p1[k, rank].astype(F32) + s2buf[k, 2].astype(F32)
        sum2[k] = total.astype(BF16)
        zt = x + 2 * k
        send(sum2.at[k], s3buf.at[z], s3_recv.at[z], 2 * zt + y, pos, zt != z)

    backward(0)
    pair_sums()
    backward(1)
    plane_sum(0)
    backward(2)

    g = dot(feat[0], ge[0], TN) + dot(feat[1], ge[1], TN)
    gain_row = jnp.sum(acc[...], axis=0, keepdims=True)
    g = jnp.where(lax.broadcasted_iota(jnp.int32, (64, d0), 0) == 31, gain_row, g)
    turned = jnp.concatenate([g, jnp.zeros_like(g)], axis=0).T
    for d in range(dp):
        low = turned[d * part0 : d * part0 + part_h, :64]
        high = turned[d * part0 + part_h : (d + 1) * part0, :64]
        small[d, :part_h, :] = jnp.concatenate([low, high], axis=1).astype(BF16)
    sums = 2.0 * dot(jnp.ones((16, half), BF16), cot[...], NN)[0:8]
    for d in range(dp):
        own = jnp.concatenate(
            [sums[:, d * part1 : (d + 1) * part1], jnp.zeros((8, 128 - part1), F32)], axis=1
        )
        small[d, part_h:, :] = jnp.concatenate([own, own], axis=0).astype(BF16)
    for j in range(1, dp):
        to = (me + j) % dp
        send(small.at[to], sbuf.at[me], small_recv.at[me], to, pos)
    sbuf[me] = small[me]
    plane_sum(1)

    for zz in range(4):
        arrive(s3buf.at[zz], s3_recv.at[zz], own_rank & (z != zz))

    @pl.when(own_rank)
    def _():
        value = sum2[z // 2].astype(F32)
        for j in range(1, 4):
            value = value + s3buf[(z + j) % 4].astype(F32)
        fin[c] = value.astype(BF16)

    send(fin.at[c], fin.at[c], fin_recv.at[c], me, across, own_rank)
    arrive(fin.at[c], fin_recv.at[c], jnp.logical_not(own_rank))
    send(fin.at[c], fin.at[c], fin_recv.at[c], me, mate)

    for j in range(1, dp):
        arrive(sbuf.at[(me + j) % dp], small_recv.at[(me + j) % dp])
    tbuf[pos] = jnp.sum(sbuf[...].astype(F32), axis=0).astype(BF16)
    for j in range(1, seq):
        send(tbuf.at[pos], tbuf.at[pos], t_recv.at[pos], me, (pos + j) % seq)

    arrive(fin.at[c2], fin_recv.at[c2])
    gw_ref[...] = fin[...].astype(F32).reshape(part0, d1) * factor
    for j in range(1, seq):
        arrive(tbuf.at[(pos + j) % seq], t_recv.at[(pos + j) % seq])
    small_out[...] = jnp.sum(tbuf[...].astype(F32), axis=0) * factor

    for copy, pred in started:
        if pred is None:
            copy.wait_send()
        else:
            pl.when(pred)(lambda copy=copy: copy.wait_send())
    pooled_out.wait()


def finish_kernel(
    kernel_width, pooled_in, gw_in, small_in, pooled, gew, geb, ggain, gw, gpb,
    turned, held, held_gw, small, out_ew, out_eb, out_gain, out_pb, load_sem, store_sem,
):
    part0, part1 = gw_in.shape[0], gpb.shape[1]
    part_h = part0 // 2
    rows = pooled_in.shape[0] // PIECES
    pieces = [(small_in, small, None), (gw_in, held_gw, gw)]
    for i in range(PIECES):
        span = pl.ds(i * rows, rows)
        pieces.append((pooled_in.at[span], held.at[span], pooled.at[span]))
    loads = [
        pltpu.make_async_copy(src, mid, load_sem.at[i]) for i, (src, mid, _) in enumerate(pieces)
    ]
    for load in loads:
        load.start()
    stores = []

    def store(src, dst):
        copy = pltpu.make_async_copy(src, dst, store_sem.at[len(stores)])
        stores.append(copy)
        copy.start()

    for load, (_, mid, dst) in zip(loads[1:], pieces[1:]):
        load.wait()
        store(mid, dst)
    loads[0].wait()
    out_pb[...] = small[part_h : part_h + 1, :part1]
    low, high = small[:part_h, :64], small[:part_h, 64:]
    channels = jnp.concatenate([low, high, jnp.zeros((128 - part0, 64), F32)], axis=0)
    turned[...] = jnp.concatenate([channels, channels], axis=1).T
    for letter in range(4):
        out_ew[:, letter, :] = turned[16 * letter : 16 * letter + kernel_width, :part0]
    out_eb[...] = turned[15:16, :part0]
    out_gain[...] = turned[31:32, :part0]
    store(out_pb, gpb)
    store(out_ew, gew)
    store(out_eb, geb)
    store(out_gain, ggain)
    for copy in stores:
        copy.wait()


def shape(dims, kind):
    return jax.ShapeDtypeStruct(dims, kind)


def fused(bases, embed_weight, embed_bias, norm_gain, proj_weight, proj_bias, cotangent):
    kernel_width = embed_weight.shape[0]
    length = bases.shape[1]
    half = length // 2
    part0, d1 = proj_weight.shape
    part1 = proj_bias.shape[0]
    dp, seq = 8, 4
    d0, part_h = part0 * dp, part0 // 2
    big = half // 3
    vmem, hbm = pl.BlockSpec(memory_space=pltpu.VMEM), pl.BlockSpec(memory_space=pl.ANY)
    dma = pltpu.SemaphoreType.DMA
    scratch = [
        ((half, d1), BF16),
        ((1, length), jnp.int32),
        (embed_weight.shape, BF16),
        ((1, part0), BF16),
        ((1, part0), BF16),
        ((1, part1), BF16),
        ((2, 128), jnp.int32),
        ((16, length), jnp.int32),
        ((length, 128), F32),
        ((2, half, 64), BF16),
        ((2, 2, big, d0), F32),
        ((2, half, d0), F32),
        ((2, half, d0), F32),
        ((2, half, 128), F32),
        ((half, d0), BF16),
        ((2, half, d0), BF16),
        ((2, big, d0), F32),
        ((2, 2, big, 128), F32),
        ((8, d0), F32),
        ((128, 128), F32),
        ((part_h + 16, 128), BF16),
        ((dp, part_h + 16, 128), BF16),
        ((dp, 2, part_h, d1), BF16),
        ((half, d1), BF16),
        ((dp, 2, part_h, d1), BF16),
        ((2, 4, part_h, d1), BF16),
        ((2, 4, part_h, d1), BF16),
        ((2, 4, part_h, d1), BF16),
        ((2, part_h, d1), BF16),
        ((4, part_h, d1), BF16),
        ((2, part_h, d1), BF16),
        ((dp, part_h + 16, 128), BF16),
        ((dp, part_h + 16, 128), BF16),
        ((seq, part_h + 16, 128), BF16),
    ]
    pooled, gw, small = pl.pallas_call(
        functools.partial(fused_kernel, kernel_width),
        out_shape=(
            shape((half, d1), BF16), shape((part0, d1), F32), shape((part_h + 16, 128), F32)
        ),
        in_specs=[hbm] * 7,
        out_specs=(hbm, vmem, vmem),
        scratch_shapes=[pltpu.VMEM(dims, kind) for dims, kind in scratch]
        + [dma((n,)) for n in (96, 2, dp)]
        + [dma((dp, 2)), dma((2,)), dma((2, 4)), dma((4,)), dma((2,)), dma((dp,)), dma((seq,)), dma((9,))],
        compiler_params=pltpu.CompilerParams(
            collective_id=0, has_side_effects=True, vmem_limit_bytes=60 * 2**20
        ),
        name="fused_step",
    )(
        bases, embed_weight, embed_bias[None], norm_gain[None], proj_weight, proj_bias[None],
        cotangent[0],
    )
    outs = pl.pallas_call(
        functools.partial(finish_kernel, kernel_width),
        out_shape=(
            shape((half, d1), BF16),
            shape(embed_weight.shape, F32),
            shape((1, part0), F32),
            shape((1, part0), F32),
            shape((part0, d1), F32),
            shape((1, part1), F32),
        ),
        in_specs=[hbm] * 3,
        out_specs=(hbm,) * 6,
        scratch_shapes=[
            pltpu.VMEM((128, 128), F32),
            pltpu.VMEM((half, d1), BF16),
            pltpu.VMEM((part0, d1), F32),
            pltpu.VMEM((part_h + 16, 128), F32),
            pltpu.VMEM(embed_weight.shape, F32),
            pltpu.VMEM((1, part0), F32),
            pltpu.VMEM((1, part0), F32),
            pltpu.VMEM((1, part1), F32),
            dma((PIECES + 2,)),
            dma((PIECES + 5,)),
        ],
        compiler_params=pltpu.CompilerParams(vmem_limit_bytes=60 * 2**20),
        name="finish_step",
    )(pooled, gw, small)
    return (outs[0][None], outs[1], outs[2][0], outs[3][0], outs[4], outs[5][0])


def with_halo(x, sides, width):
    for axis, dim in sides:
        devices, length = (lax.axis_size(axis), x.shape[dim])
        up = [(i, (i + 1) % devices) for i in range(devices - 1)]
        down = [(j, i) for i, j in up]
        last = lax.slice_in_dim(x, length - width, length, axis=dim)
        leading = lax.slice_in_dim(x, 0, width, axis=dim)
        before = lax.ppermute(last, axis, up)
        after = lax.ppermute(leading, axis, down)
        x = jnp.concatenate([before, x, after], axis=dim)
    return x


def plain(bases, embed_weight, embed_bias, norm_gain, proj_weight, proj_bias, cotangent):
    kernel_width = embed_weight.shape[0]
    row_count = bases.shape[1]
    codes = bases + 1
    padded = with_halo(codes, (("seq", 1),), kernel_width // 2)[0]
    full_embed, full_bias, full_gain, full_proj, full_proj_bias = (
        lax.all_gather(embed_weight, "dp", axis=2, tiled=True),
        lax.all_gather(embed_bias, "dp", axis=0, tiled=True),
        lax.all_gather(norm_gain, "dp", axis=0, tiled=True),
        lax.all_gather(proj_weight, "dp", axis=0, tiled=True),
        lax.all_gather(proj_bias, "dp", axis=0, tiled=True),
    )
    letters = jnp.arange(1, 5, dtype=jnp.int32)
    features = jnp.concatenate(
        [
            (padded[k : k + row_count, None] == letters).astype(jnp.bfloat16)
            for k in range(kernel_width)
        ],
        axis=1,
    )
    flat_weight = full_embed.reshape(kernel_width * 4, -1)
    embedded = (
        jnp.dot(features, flat_weight, preferred_element_type=jnp.float32)
        + full_bias.astype(jnp.float32)
    ).astype(jnp.bfloat16)
    values = embedded.astype(jnp.float32)
    inverse = lax.rsqrt(jnp.mean(values * values, axis=1, keepdims=True) + 1e-06)
    scaled = values * inverse
    normed = scaled * full_gain.astype(jnp.float32)
    activated = jax.nn.gelu(normed, approximate=True).astype(jnp.bfloat16)
    product = jnp.dot(activated, full_proj, preferred_element_type=jnp.float32)
    mixed = product + full_proj_bias.astype(jnp.float32)
    pooled = jnp.mean(mixed.reshape(row_count // 2, 2, -1), axis=1).astype(jnp.bfloat16)
    scale_factor = 0.5 / (row_count * lax.axis_size("seq") * lax.axis_size("dp"))
    grad_mixed = (jnp.repeat(cotangent[0].astype(jnp.float32), 2, axis=0) * scale_factor).astype(
        jnp.bfloat16
    )
    grad_proj_weight = lax.dot_general(
        activated, grad_mixed, (((0,), (0,)), ((), ())), preferred_element_type=jnp.float32
    )
    grad_proj_bias = jnp.sum(grad_mixed.astype(jnp.float32), axis=0)
    grad_activated = lax.dot_general(
        grad_mixed, full_proj, (((1,), (1,)), ((), ())), preferred_element_type=jnp.float32
    )
    _, pullback = jax.vjp(lambda v: jax.nn.gelu(v, approximate=True), normed)
    grad_normed = pullback(grad_activated)[0]
    grad_norm_gain = jnp.sum(grad_normed * scaled, axis=0)
    weighted = grad_normed * full_gain.astype(jnp.float32)
    grad_embedded = (
        inverse * (weighted - scaled * jnp.mean(weighted * scaled, axis=1, keepdims=True))
    ).astype(jnp.bfloat16)
    grad_embed_weight = lax.dot_general(
        features, grad_embedded, (((0,), (0,)), ((), ())), preferred_element_type=jnp.float32
    ).reshape(kernel_width, 4, -1)
    grad_embed_bias = jnp.sum(grad_embedded.astype(jnp.float32), axis=0)
    whole = lax.psum(
        (grad_embed_weight, grad_embed_bias, grad_norm_gain, grad_proj_weight, grad_proj_bias),
        "seq",
    )
    results = (
        lax.psum_scatter(whole[0], "dp", scatter_dimension=2, tiled=True),
        lax.psum_scatter(whole[1], "dp", scatter_dimension=0, tiled=True),
        lax.psum_scatter(whole[2], "dp", scatter_dimension=0, tiled=True),
        lax.psum_scatter(whole[3], "dp", scatter_dimension=0, tiled=True),
        lax.psum_scatter(whole[4], "dp", scatter_dimension=0, tiled=True),
    )
    return (pooled[None], results[0], results[1], results[2], results[3], results[4])


def solution(mesh):
    placed = (
        P("dp", "seq"),
        P(None, None, "dp"),
        P("dp"),
        P("dp"),
        P("dp", None),
        P("dp"),
        P("dp", "seq", None),
    )
    step = fused if (mesh.shape["dp"], mesh.shape["seq"]) == (8, 4) else plain
    return jax.shard_map(
        step,
        mesh=mesh,
        in_specs=placed,
        out_specs=(
            P("dp", "seq", None),
            P(None, None, "dp"),
            P("dp"),
            P("dp"),
            P("dp", None),
            P("dp"),
        ),
        check_vma=False,
    )
```
